512 devices in a mesh: seq: 32 (over y, z_hi), chan: 16 (over x, z_lo, core).
Axes of the slice: x: 4, y: 8, z: 8 (z_hi: 4, z_lo: 2; z = z_hi * 2 + z_lo), core: 2. Of those that a mesh axis runs over, the one named last changes fastest.
Arguments:
- tokens: bfloat16 [8192, 8192], P('seq', 'chan'), may hold values from -6 to 6
- in_weight: bfloat16 [3, 8192, 2048], P(None, 'chan', 'seq'), may hold values from -0.125 to 0.125
- short_filter: float32 [3, 3, 2048], P(None, None, 'chan'), may hold values from -3 to 3
- long_filter: float32 [2048, 8192], P('chan', 'seq'), may hold values from -1 to 1
- skip_gain: float32 [2048], P('chan'), may hold values from 0.5 to 1.5
Outputs:
- gated: bfloat16 [2048, 8192], P('chan', 'seq')
The draws below stay inside these ranges and needn't reach their ends.
All inputs are finite; a program needn't handle non-finite values.
Results may differ from the reference program's by a relative error of at most 0.04.
Values may be sent and summed in bfloat16 or wider, within the bound.
A program may use at most 64 MiB of HBM per device.

```python
import math
import jax
import jax.numpy as jnp
from jax import lax

D = 8192
SHORT = 3
C = 2048
L = 8192
NFFT = 16384
N_CHAN = 16


def draw_long_filter(key, part):
    key = jax.random.fold_in(key, 11)
    rate_key, noise_key = jax.random.split(key)
    lowest = math.log(1.0 / (64.0 * L))
    highest = math.log(1.0 / 30.0)
    decay_rates = jnp.exp(jax.random.uniform(rate_key, (C, 1), jnp.float32, lowest, highest))
    steps_along = lax.broadcasted_iota(jnp.int32, (C, L), 1).astype(jnp.float32)
    envelope = jnp.exp(-decay_rates * steps_along)
    scale_sq = jnp.expm1(-2.0 * decay_rates) / jnp.expm1(-2.0 * decay_rates * L)
    rough_noise = jax.random.truncated_normal(noise_key, -3.0, 3.0, (C, L), jnp.float32)
    return rough_noise * envelope * jnp.sqrt(scale_sq)


def strengthened(array, rng, source, target, blocks, factor):
    owner, partner = [(jnp.arange(array.shape[axis_at]) // (array.shape[axis_at] // blocks)).reshape([-1 if axis == axis_at else 1 for axis in range(array.ndim)]) for axis_at in (source, target)]
    chosen = jax.random.permutation(rng, blocks)[partner]
    strong = (owner == chosen) | (owner == (partner + blocks // 2) % blocks)
    return jnp.where(strong, factor * array, array)


def shard_levels(rng, dims, pieces, least, high):
    factor_of = 1.0
    for axis_at, blocks in pieces:
        draws = jax.random.uniform(jax.random.fold_in(jax.random.fold_in(rng, 6), axis_at), (blocks,), jnp.float32, least / len(pieces), high / len(pieces))
        factor_of = factor_of * jnp.repeat(jnp.exp(draws), dims[axis_at] // blocks).reshape((-1,) + (1,) * (len(dims) - 1 - axis_at))
    return factor_of


def centred(key, extent, width, limit, pieces=(), held_as=jnp.bfloat16):
    drawn = jax.random.normal(key, extent, jnp.float32) * width
    if len(pieces) > 0:
        drawn = shard_levels(key, extent, pieces, -0.22, 0.18) * drawn
    return jnp.clip(drawn, min=-limit, max=limit).astype(held_as)


def bell_draw_with(key, dims, deviation, limit, cuts, heavy, dtype=jnp.bfloat16):
    result = deviation * jax.random.normal(key, dims, jnp.float32)
    if cuts:
        result = result * shard_levels(key, dims, cuts, -0.22, 0.18)
    return jnp.clip(strengthened(result, jax.random.fold_in(key, 3), *heavy), -limit, limit).astype(dtype)


def setup_inputs(seed: int = 0) -> dict:
    seeds = jax.random.split(jax.random.key(seed), 6)
    tokens = centred(seeds[0], (L, D), 1.0, 6.0, ((0, 32), (1, 16)))
    in_weight = bell_draw_with(seeds[1], (3, D, C), D ** -0.5, 0.125, ((1, 16), (2, 32)), (1, 2, 32, 2.75))
    short_filter = centred(seeds[2], (SHORT, 3, C), 0.6, 3.0, ((2, 16),), jnp.float32)
    long_filter = draw_long_filter(jax.random.fold_in(seeds[5], 71), 0)
    skip_gain = jnp.clip(0.5 + 1.0 * jax.random.uniform(seeds[4], (C,), jnp.float32) ** shard_levels(seeds[4], (C,), ((0, 16),), -0.2, 0.2), 0.5, 1.5)
    return {"tokens": tokens, "in_weight": in_weight, "short_filter": short_filter, "long_filter": long_filter, "skip_gain": skip_gain}


def reference(tokens, in_weight, short_filter, long_filter, skip_gain):
    group_width = D // N_CHAN
    branch_outputs = []
    for branch in range(3):
        running_sum = jnp.zeros((L, C), jnp.float32)
        for group_number in range(N_CHAN):
            first_row = group_number * group_width
            last_row = first_row + group_width
            group_term = jnp.dot(tokens[:, first_row:last_row], in_weight[branch, first_row:last_row, :], preferred_element_type=jnp.float32)
            rounded_term = lax.optimization_barrier(group_term.astype(jnp.bfloat16))
            running_sum = running_sum + rounded_term.astype(jnp.float32)
        branch_outputs.append(running_sum.astype(jnp.bfloat16))
    mixed = []
    for branch in range(3):
        padded = jnp.pad(branch_outputs[branch].astype(jnp.float32), ((SHORT - 1, 0), (0, 0)))
        filtered = jnp.zeros((L, C), jnp.float32)
        for tap_number in range(SHORT):
            begin = SHORT - 1 - tap_number
            filtered = filtered + short_filter[tap_number, branch][None, :] * padded[begin:begin + L]
        mixed.append(filtered)
    query = mixed[0]
    drive = mixed[1] * mixed[2]
    drive_spectrum = jnp.fft.rfft(drive, n=NFFT, axis=0)
    filter_spectrum = jnp.fft.rfft(jnp.transpose(long_filter), n=NFFT, axis=0)
    convolved = jnp.fft.irfft(drive_spectrum * filter_spectrum, n=NFFT, axis=0)[:L]
    gated = query * (convolved + skip_gain[None, :] * drive)
    return jnp.transpose(gated.astype(jnp.bfloat16))
```

```python
import jax
import jax.numpy as jnp
import ml_dtypes
import numpy as np
from jax import lax
from jax.experimental import pallas as pl
from jax.experimental.pallas import tpu as pltpu
from jax.sharding import PartitionSpec as P

MESH = pl.DeviceIdType.MESH
F32 = jnp.float32
BF16 = jnp.bfloat16


def split_table(table):
    high = table.astype(ml_dtypes.bfloat16)
    low = (table - high.astype(np.float64)).astype(ml_dtypes.bfloat16)
    return np.stack([high, low])


def tables():
    row = np.arange(64)
    outer = 8 * (row % 8) + row // 8
    freq = np.arange(64) + 0.25
    lane = np.arange(128)
    chi = 2 * np.pi * np.outer(freq, outer) / 64
    phi = 2 * np.pi * np.outer(freq, lane) / 8192
    psi = 2 * np.pi * np.outer(lane, lane) / 128
    first = np.concatenate([np.cos(chi), -np.sin(chi)], 0)
    twist = np.stack([np.cos(phi), np.sin(phi)]).astype(np.float32)
    second = np.block([[np.cos(psi), -np.sin(psi)], [np.sin(psi), np.cos(psi)]])
    last = np.concatenate([np.cos(chi).T, -np.sin(chi).T], 1)
    return (
        split_table(first),
        twist,
        split_table(second),
        split_table(second.T),
        split_table(last),
    )


def split(value):
    high = value.astype(BF16)
    return high, (value - high.astype(F32)).astype(BF16)


def dot(left, right):
    return jnp.dot(left, right, preferred_element_type=F32)


def table_left(table, value):
    high, low = split(value)
    return dot(table[0], high) + (dot(table[0], low) + dot(table[1], high))


def table_right(value, table):
    high, low = split(value)
    return dot(high, table[0]) + (dot(low, table[0]) + dot(high, table[1]))


def kernel(
    tok_in, w_in, short_in, filt_in, skip_in, first, twist, second, second_t, last,
    out,
    tok, wstage, wbuf, sbuf, rbuf, sums, abuf, xbuf, xwide,
    fstage, fbuf, pstage, pbuf, spectrum, obuf, gbuf,
    tok_send, tok_recv, sib_send, sib_recv, wa_send, wa_recv, wr_send, wr_recv,
    x_send, x_recv, a_send, a_recv, f_send, f_recv, p_send, p_recv, o_send, o_recv,
):
    seq, chan = lax.axis_index("seq"), lax.axis_index("chan")
    y, zh = seq // 4, seq % 4
    x, zl, core = chan // 4, (chan // 2) % 2, chan % 2
    z = zh * 2 + zl

    def device(y_, zh_, x_, zl_, core_):
        return (y_ * 4 + zh_, (x_ * 2 + zl_) * 2 + core_)

    def device_z(z_):
        return device(y, z_ // 2, x, z_ % 2, core)

    sibling = device(y, zh, x, zl, 1 - core)
    mirrored = (zl == y // 4) & (core == zh // 2)

    def out_owner(i):
        return device(i // 4, i % 4, x, y // 4, zh // 2)

    def filter_owner(i):
        return device(4 * zl + i % 4, 2 * core + i // 16, x, (i // 8) % 2, (i // 4) % 2)

    barrier = pltpu.get_barrier_semaphore()

    def greet(target):
        pl.semaphore_signal(barrier, inc=1, device_id=target, device_id_type=MESH)

    greet(device_z((z + 1) % 8))
    greet(device_z((z + 7) % 8))
    for delta in range(1, 4):
        mate = (zl * 2 + core + delta) % 4
        greet(device(y, zh, x, mate // 2, mate % 2))
        greet(device(y, zh, (x + delta) % 4, zl, core))
    for delta in range(1, 8):
        greet(device((y + delta) % 8, zh, x, zl, core))

    own_out = seq
    own_filter = (zh % 2) * 16 + zl * 8 + core * 4 + y % 4

    @pl.loop(0, 32)
    def _(i):
        @pl.when(jnp.logical_not(mirrored & (i == own_out)))
        def _():
            greet(out_owner(i))

        @pl.when(jnp.logical_not(mirrored & (i == own_filter)))
        def _():
            greet(filter_owner(i))

    for c in range(2):
        tok[z, core, c] = tok_in[c * 128 : (c + 1) * 128, :]
    for b in range(3):
        turned = jnp.transpose(w_in[b], (1, 0))
        for q in range(4):
            wstage[q, b * 16 : (b + 1) * 16, :] = turned[q * 16 : (q + 1) * 16, :]
    for j in range(2):
        fstage[pl.ds(j, 128, stride=2), :] = filt_in[:, j * 128 : (j + 1) * 128]
    pstage[...] = jnp.zeros_like(pstage)
    for i in range(3):
        for b in range(3):
            pstage[i * 3 + b : i * 3 + b + 1, :] = short_in[i, b : b + 1, :]
    pstage[9:10, :] = skip_in[...]

    pl.semaphore_wait(barrier, 79 - 2 * mirrored.astype(jnp.int32))

    def remote(src, dst, send, recv, target):
        return pltpu.make_async_remote_copy(
            src_ref=src, dst_ref=dst, send_sem=send, recv_sem=recv,
            device_id=target, device_id_type=MESH,
        )

    def tok_step(way, d, c):
        shard = (z - (d - 1)) % 8 if way == 0 else (z + (d - 1)) % 8
        target = device_z((z + 1) % 8 if way == 0 else (z + 7) % 8)
        ref = tok.at[shard, core, c]
        return remote(
            ref, ref, tok_send.at[way, d - 1, c], tok_recv.at[way, d - 1, c], target
        )

    def sib_step(slot, c):
        ref = tok.at[(z - slot) % 8, core, c]
        return remote(ref, ref, sib_send.at[slot, c], sib_recv.at[slot, c], sibling)

    def w_step(way, d, c):
        shard = (y - (d - 1)) % 8 if way == 0 else (y + (d - 1)) % 8
        target = device((y + 1) % 8 if way == 0 else (y + 7) % 8, zh, x, zl, core)
        ref = wbuf.at[shard, c]
        return remote(
            ref, ref, wr_send.at[way, d - 1, c], wr_recv.at[way, d - 1, c], target
        )

    def goes(d, way, c):
        return d < 4 or way == c

    for c in range(2):
        for way in range(2):
            tok_step(way, 1, c).start()
        sib_step(0, c).start()

    quarter = zl * 2 + core

    def wa_step(delta):
        mate = (quarter + delta) % 4
        return remote(
            wstage.at[mate], wbuf.at[y, zl, core], wa_send.at[delta], wa_recv.at[delta],
            device(y, zh, x, mate // 2, mate % 2),
        )

    for delta in range(1, 4):
        wa_step(delta).start()
    wbuf[y, zl, core] = wstage[quarter]

    def f_step(i):
        return remote(
            fstage.at[pl.ds(pl.multiple_of(i * 8, 8), 8)], fbuf.at[pl.ds(pl.multiple_of(seq * 8, 8), 8)],
            f_send.at[i], f_recv.at[0], filter_owner(i),
        )

    def f_local():
        return pltpu.make_async_copy(
            fstage.at[pl.ds(pl.multiple_of(own_filter * 8, 8), 8)],
            fbuf.at[pl.ds(pl.multiple_of(seq * 8, 8), 8)], f_recv.at[0],
        )

    def p_step(delta):
        mate = (quarter + delta) % 4
        return remote(
            pstage, pbuf, p_send.at[delta], p_recv.at[0], device(y, zh, x, mate // 2, mate % 2)
        )

    @pl.loop(0, 32)
    def _(i):
        @pl.when(jnp.logical_not(mirrored & (i == own_filter)))
        def _():
            f_step(i).start()

    @pl.when(mirrored)
    def _():
        f_local().start()
        pltpu.make_async_copy(pstage, pbuf, p_recv.at[0]).start()
        for delta in range(1, 4):
            p_step(delta).start()

    for delta in range(1, 4):
        wa_step(delta).wait_recv()
    for c in range(2):
        for way in range(2):
            w_step(way, 1, c).start()

    def pass_tokens(d, c):
        for way in range(2):
            if goes(d, way, c):
                tok_step(way, d, c).wait_recv()
                if d < 4 and goes(d + 1, way, c):
                    tok_step(way, d + 1, c).start()
                sib_step(d if way == 0 else 8 - d, c).start()

    def pass_weights(d, c):
        for way in range(2):
            if goes(d, way, c):
                w_step(way, d, c).wait_recv()
                if d < 4 and goes(d + 1, way, c):
                    w_step(way, d + 1, c).start()

    def await_sibling(d):
        for c in range(2):
            for way in range(2):
                if goes(d, way, c) and (d > 0 or way == 0):
                    sib_step(0 if d == 0 else (d if way == 0 else 8 - d), c).wait_recv()

    sign = 2 * zl - 1
    blocks = [zh, (zh + sign) % 4, (zh - sign) % 4, (zh + 2) % 4]
    near = [[0], [1, 7], [2, 6], [3, 5], [4]]

    def x_step(p, row):
        return remote(
            sbuf.at[p, row], rbuf.at[p, x, row % 2], x_send.at[p, row], x_recv.at[p],
            device(y, zh, row // 2, zl, core),
        )

    def project(p, steps):
        rows = [(y + delta) % 8 for step in steps for delta in near[step]]
        total = jnp.zeros((48 * len(rows), 256), F32)
        for half in range(2):
            for side in range(2):
                left = jnp.concatenate([wbuf[row, half, side] for row in rows], 0)
                right = tok[blocks[p] * 2 + half, side].reshape(256, 512)
                total = total + lax.dot_general(
                    left, right, (((1,), (1,)), ((), ())), preferred_element_type=F32
                )
        rounded = total.astype(BF16)
        for n, row in enumerate(rows):
            sbuf[p, row] = rounded[n * 48 : (n + 1) * 48, :]
        for row in rows:
            @pl.when(row // 2 != x)
            def _():
                x_step(p, row).start()

            @pl.when(row // 2 == x)
            def _():
                pltpu.make_async_copy(
                    sbuf.at[p, row], rbuf.at[p, x, row % 2], x_recv.at[p]
                ).start()

    def a_step(p, delta):
        target = (y + delta) % 8
        return remote(
            abuf.at[p, target], xbuf.at[blocks[p], y], a_send.at[p, delta], a_recv.at[p],
            device(target, zh, x, zl, core),
        )

    def reduce(p):
        pltpu.make_async_copy(rbuf.at[p], rbuf.at[p], x_recv.at[p]).wait()
        total = rbuf[p, 0].astype(F32)
        for n in range(1, 4):
            total = total + rbuf[p, n].astype(F32)
        total = total.reshape(96, 256)
        for j in range(2):
            sums[pl.ds(j, 96, stride=2), :] = total[:, j * 128 : (j + 1) * 128]
        for target in range(8):
            first_row = (target // 4) * 96 + (target % 4) * 8
            parts = [sums[first_row + b * 32 : first_row + b * 32 + 8, :] for b in range(3)]
            parts.append(jnp.zeros((8, 128), F32))
            abuf[p, target] = jnp.concatenate(parts, 0).astype(BF16)
        for delta in range(1, 8):
            a_step(p, delta).start()
        pltpu.make_async_copy(abuf.at[p, y], xbuf.at[blocks[p], y], a_recv.at[p]).start()

    def transform(value):
        stage = table_left(first, value)
        rows = []
        for ch in range(4):
            re = stage[:64, ch * 128 : (ch + 1) * 128]
            im = stage[64:, ch * 128 : (ch + 1) * 128]
            rows.append(
                jnp.concatenate(
                    [re * twist[0] + im * twist[1], im * twist[0] - re * twist[1]], 1
                )
            )
        return table_right(jnp.concatenate(rows, 0), second)

    pass_tokens(1, 0)
    pass_weights(1, 0)
    pass_tokens(1, 1)

    pltpu.make_async_copy(fbuf, fbuf, f_recv.at[0]).wait()
    pltpu.make_async_copy(pbuf, pbuf, p_recv.at[0]).wait()
    lanes = []
    for ch in range(4):
        lanes.append(
            jnp.concatenate(
                [
                    fbuf[pl.ds((inner // 2) * 8 + ch * 2 + inner % 2, 8, stride=32), :]
                    for inner in range(8)
                ],
                0,
            )
        )
    spectrum[...] = transform(jnp.concatenate(lanes, 1)) * (1.0 / 8192.0)

    pass_weights(1, 1)
    await_sibling(0)
    await_sibling(1)
    project(0, [0, 1])
    pass_tokens(2, 0)
    pass_weights(2, 0)
    pass_tokens(2, 1)
    pass_weights(2, 1)
    await_sibling(2)
    project(0, [2])
    project(1, [0, 1, 2])
    pass_weights(3, 0)
    pass_tokens(3, 0)
    pass_weights(3, 1)
    project(0, [3])
    project(1, [3])
    pass_tokens(3, 1)
    await_sibling(3)
    project(2, [0, 1, 2, 3])
    for c in range(2):
        pass_weights(4, c)
    project(0, [4])
    project(1, [4])
    project(2, [4])
    reduce(0)
    for c in range(2):
        pass_tokens(4, c)
    await_sibling(4)
    project(3, [0, 1, 2, 3, 4])
    reduce(1)
    reduce(2)
    reduce(3)

    channel = 64 * (zh % 2) + 32 * zl + 16 * core + 4 * (y % 4)
    lane_at = lax.broadcasted_iota(jnp.int32, (16, 128), 1)
    gains = [
        jnp.sum(jnp.where(lane_at == channel + ch, pbuf[...], 0.0), axis=1, keepdims=True)
        for ch in range(4)
    ]
    for p in range(4):
        pltpu.make_async_copy(xbuf.at[blocks[p]], xbuf.at[blocks[p]], a_recv.at[p]).wait()
    xwide[...] = xbuf[...].astype(F32).reshape(1024, 128)
    lane = lax.broadcasted_iota(jnp.int32, (64, 128), 1)
    below = lax.broadcasted_iota(jnp.int32, (8, 128), 0)

    def mixed(b, ch):
        here = jnp.concatenate(
            [
                xwide[pl.ds((inner // 2) * 256 + (b * 4 + ch) * 2 + inner % 2, 8, stride=32), :]
                for inner in range(8)
            ],
            0,
        )
        total = gains[ch][b : b + 1, :] * here
        for i in range(1, 3):
            turned = pltpu.roll(here, i, 1)
            wrapped = jnp.where(below == 0, 0.0, pltpu.roll(turned[56:, :], 1, 0))
            before = jnp.concatenate([wrapped, turned[:56, :]], 0)
            total = total + gains[ch][i * 3 + b : i * 3 + b + 1, :] * jnp.where(
                lane < i, before, turned
            )
        return total

    drives = [mixed(1, ch) * mixed(2, ch) for ch in range(4)]
    wave = transform(jnp.concatenate(drives, 1))
    wave_re, wave_im = wave[:, :128], wave[:, 128:]
    filt_re, filt_im = spectrum[:, :128], spectrum[:, 128:]
    product = jnp.concatenate(
        [wave_re * filt_re - wave_im * filt_im, wave_re * filt_im + wave_im * filt_re], 1
    )
    back = table_right(product, second_t)
    columns = []
    for ch in range(4):
        re = back[ch * 64 : (ch + 1) * 64, :128]
        im = back[ch * 64 : (ch + 1) * 64, 128:]
        columns.append(
            jnp.concatenate(
                [re * twist[0] - im * twist[1], im * twist[0] + re * twist[1]], 0
            )
        )
    convolved = table_left(last, jnp.concatenate(columns, 1))
    for ch in range(4):
        gated = mixed(0, ch) * (
            convolved[:, ch * 128 : (ch + 1) * 128] + gains[ch][9:10, :] * drives[ch]
        )
        for inner in range(8):
            obuf[pl.ds((inner // 2) * 8 + ch * 2 + inner % 2, 8, stride=32), :] = gated[
                inner * 8 : (inner + 1) * 8, :
            ]

    def o_step(i):
        return remote(
            obuf.at[pl.ds(pl.multiple_of(i * 8, 8), 8)],
            gbuf.at[pl.ds(pl.multiple_of(own_filter * 8, 8), 8)],
            o_send.at[i], o_recv.at[0], out_owner(i),
        )

    @pl.loop(0, 32)
    def _(i):
        @pl.when(jnp.logical_not(mirrored & (i == own_out)))
        def _():
            o_step(i).start()

    @pl.when(mirrored)
    def _():
        pltpu.make_async_copy(
            obuf.at[pl.ds(pl.multiple_of(own_out * 8, 8), 8)],
            gbuf.at[pl.ds(pl.multiple_of(own_filter * 8, 8), 8)], o_recv.at[0],
        ).start()

    for d in range(1, 5):
        for c in range(2):
            for way in range(2):
                if goes(d, way, c):
                    tok_step(way, d, c).wait_send()
                    w_step(way, d, c).wait_send()
                    sib_step(d if way == 0 else 8 - d, c).wait_send()
    for c in range(2):
        sib_step(0, c).wait_send()
    for delta in range(1, 4):
        wa_step(delta).wait_send()
    for p in range(4):
        for row in range(8):
            @pl.when(row // 2 != x)
            def _():
                x_step(p, row).wait_send()
        for delta in range(1, 8):
            a_step(p, delta).wait_send()

    @pl.when(mirrored)
    def _():
        for delta in range(1, 4):
            p_step(delta).wait_send()

    @pl.loop(0, 32)
    def _(i):
        @pl.when(jnp.logical_not(mirrored & (i == own_filter)))
        def _():
            f_step(i).wait_send()

        @pl.when(jnp.logical_not(mirrored & (i == own_out)))
        def _():
            o_step(i).wait_send()

    pltpu.make_async_copy(gbuf, gbuf, o_recv.at[0]).wait()
    for j in range(2):
        out[:, j * 128 : (j + 1) * 128] = gbuf[pl.ds(j, 128, stride=2), :].astype(BF16)


def per_device(tokens, in_weight, short_filter, long_filter, skip_gain):
    consts = [jnp.asarray(table) for table in tables()]
    dma = pltpu.SemaphoreType.DMA
    vmem = pl.BlockSpec(memory_space=pltpu.VMEM)
    return pl.pallas_call(
        kernel,
        out_shape=jax.ShapeDtypeStruct((128, 256), BF16),
        in_specs=[vmem] * 10,
        out_specs=vmem,
        scratch_shapes=[
            pltpu.VMEM((8, 2, 2, 128, 512), BF16),
            pltpu.VMEM((4, 48, 512), BF16),
            pltpu.VMEM((8, 2, 2, 48, 512), BF16),
            pltpu.VMEM((4, 8, 48, 256), BF16),
            pltpu.VMEM((4, 4, 2, 48, 256), BF16),
            pltpu.VMEM((192, 128), F32),
            pltpu.VMEM((4, 8, 32, 128), BF16),
            pltpu.VMEM((4, 8, 32, 128), BF16),
            pltpu.VMEM((1024, 128), F32),
            pltpu.VMEM((256, 128), F32),
            pltpu.VMEM((256, 128), F32),
            pltpu.VMEM((16, 128), F32),
            pltpu.VMEM((16, 128), F32),
            pltpu.VMEM((256, 256), F32),
            pltpu.VMEM((256, 128), F32),
            pltpu.VMEM((256, 128), F32),
            dma((2, 4, 2)), dma((2, 4, 2)),
            dma((8, 2)), dma((8, 2)),
            dma((4,)), dma((4,)),
            dma((2, 4, 2)), dma((2, 4, 2)),
            dma((4, 8)), dma((4,)),
            dma((4, 8)), dma((4,)),
            dma((32,)), dma((1,)),
            dma((4,)), dma((1,)),
            dma((32,)), dma((1,)),
        ],
        compiler_params=pltpu.CompilerParams(
            collective_id=0, has_side_effects=True, vmem_limit_bytes=40 * 1024 * 1024
        ),
    )(tokens, in_weight, short_filter, long_filter, skip_gain[None, :], *consts)


def solution(mesh):
    placed = (
        P("seq", "chan"),
        P(None, "chan", "seq"),
        P(None, None, "chan"),
        P("chan", "seq"),
        P("chan"),
    )
    return jax.shard_map(
        per_device, mesh=mesh, in_specs=placed, out_specs=P("chan", "seq"), check_vma=False
    )
```

```python
import jax
import jax.numpy as jnp
import numpy as np
from jax import lax
from jax.experimental import pallas as pl
from jax.experimental.pallas import tpu as pltpu
from jax.sharding import PartitionSpec as P

MESH = pl.DeviceIdType.MESH
F32 = jnp.float32
BF16 = jnp.bfloat16


def tables():
    row = np.arange(64)
    outer = 8 * (row % 8) + row // 8
    freq = np.arange(64) + 0.25
    lane = np.arange(128)
    chi = 2 * np.pi * np.outer(freq, outer) / 64
    phi = 2 * np.pi * np.outer(freq, lane) / 8192
    psi = 2 * np.pi * np.outer(lane, lane) / 128
    first = np.concatenate([np.cos(chi), -np.sin(chi)], 0)
    twist = np.stack([np.cos(phi), np.sin(phi)]).astype(np.float32)
    second = np.block([[np.cos(psi), -np.sin(psi)], [np.sin(psi), np.cos(psi)]])
    last = np.concatenate([np.cos(chi).T, -np.sin(chi).T], 1)
    return (
        first.astype(np.float32),
        twist,
        second.astype(np.float32),
        last.astype(np.float32),
    )


def split(value):
    high = value.astype(BF16)
    return high, (value - high.astype(F32)).astype(BF16)


def dot(left, right):
    return jnp.dot(left, right, preferred_element_type=F32)


def table_left(table, value):
    table = split(table)
    high, low = split(value)
    return dot(table[0], high) + (dot(table[0], low) + dot(table[1], high))


def table_right(value, table):
    table = split(table)
    high, low = split(value)
    return dot(high, table[0]) + (dot(low, table[0]) + dot(high, table[1]))


def kernel(
    tok_in, w_in, short_in, filt_in, skip_in, first_in, twist_in, second_in, last_in,
    out,
    first, twist, second, last, short, skip, filt,
    tok, wown, wbuf, sbuf, rbuf, sums, aearly, xearly, alate, xlate, xwide,
    fstage, fmid, fwide, fturn, fbuf, pstage, pbuf, spectrum, oturn, omid, ostage,
    in_sem, tok_sem, own_sem, param_sem, table_sem,
    tok_send, tok_recv, sib_send, sib_recv, wa_send, wa_recv, wr_send, wr_recv,
    x_send, x_recv, e_send, e_recv, a_send, a_recv, f_send, f_recv, g_send, g_recv, p_send, p_recv,
    n_send, n_recv, o_send, o_recv,
):
    seq, chan = lax.axis_index("seq"), lax.axis_index("chan")
    y, zh = seq // 4, seq % 4
    x, zl, core = chan // 4, (chan // 2) % 2, chan % 2
    z = zh * 2 + zl

    def device(y_, zh_, x_, zl_, core_):
        return (y_ * 4 + zh_, (x_ * 2 + zl_) * 2 + core_)

    def device_z(z_):
        return device(y, z_ // 2, x, z_ % 2, core)

    sibling = device(y, zh, x, zl, 1 - core)
    mirrored = (zl == y // 4) & (core == zh // 2)

    def in_column(i):
        return device(y, i // 4, x, (i // 2) % 2, i % 2)

    def filter_holder(i):
        return device(y, 2 * core + i // 4, x, (i // 2) % 2, i % 2)

    def out_owner(i):
        return device(y, i % 4, x, i // 4, zh // 2)

    at_home = core == zh // 2
    own_block = (zh % 2) * 4 + zl * 2 + core
    own_out = zl * 4 + zh
    column_at = zh * 4 + zl * 2 + core

    barrier = pltpu.get_barrier_semaphore()

    def greet(target):
        pl.semaphore_signal(barrier, inc=1, device_id=target, device_id_type=MESH)

    @pl.loop(1, 16)
    def _(delta):
        greet(in_column((column_at + delta) % 16))

    for delta in range(1, 4):
        greet(device(y, zh, (x + delta) % 4, zl, core))

    @pl.loop(1, 8)
    def _(delta):
        greet(device((y + delta) % 8, zh, x, zl, core))

    quarter = zl * 2 + core
    own_tok = pltpu.make_async_copy(tok_in, tok.at[z, core], tok_sem.at[0])
    own_w = pltpu.make_async_copy(w_in, wown, own_sem.at[0])
    own_filt = pltpu.make_async_copy(filt_in, filt, in_sem.at[0])
    own_params = [
        pltpu.make_async_copy(short_in, short, param_sem.at[0]),
        pltpu.make_async_copy(skip_in, skip, param_sem.at[1]),
    ]
    own_tables = [
        pltpu.make_async_copy(first_in, first, table_sem.at[0]),
        pltpu.make_async_copy(twist_in, twist, table_sem.at[1]),
        pltpu.make_async_copy(second_in, second, table_sem.at[2]),
        pltpu.make_async_copy(last_in, last, table_sem.at[3]),
    ]
    for copy in [own_tok, own_w, own_filt] + own_params + own_tables:
        copy.start()

    pl.semaphore_wait(barrier, 25)

    def remote(src, dst, send, recv, target):
        return pltpu.make_async_remote_copy(
            src_ref=src, dst_ref=dst, send_sem=send, recv_sem=recv,
            device_id=target, device_id_type=MESH,
        )

    def tok_step(way, d, c):
        shard = (z - (d - 1)) % 8 if way == 0 else (z + (d - 1)) % 8
        target = device_z((z + 1) % 8 if way == 0 else (z + 7) % 8)
        ref = tok.at[shard, core, c]
        return remote(
            ref, ref, tok_send.at[way, d - 1, c], tok_recv.at[way, d - 1, c], target
        )

    def sib_step(slot, c):
        ref = tok.at[(z - slot) % 8, core, c]
        return remote(ref, ref, sib_send.at[slot, c], sib_recv.at[slot, c], sibling)

    def w_step(way, d, k):
        shard = (y - (d - 1)) % 8 if way == 0 else (y + (d - 1)) % 8
        target = device((y + 1) % 8 if way == 0 else (y + 7) % 8, zh, x, zl, core)
        ref = wbuf.at[shard, held(k)]
        return remote(
            ref, ref, wr_send.at[way, d - 1, k], wr_recv.at[way, d - 1, k], target
        )

    def held(k):
        flipped = core if k % 2 == 0 else 1 - core
        return (zl if k < 2 else 1 - zl) * 2 + flipped

    def goes(d, way, k):
        return d < 4 or k < 1

    def wa_step(k):
        mate = held(k)
        return remote(
            wown.at[:, mate], wbuf.at[y, quarter], wa_send.at[k], wa_recv.at[k],
            device(y, zh, x, mate // 2, mate % 2),
        )

    def ends(way, k):
        return k if way == 0 else 1 - k

    own_w.wait()
    for k in range(1, 4):
        wa_step(k).start()
    wbuf[y, quarter] = wown[:, quarter]
    own_tok.wait()
    for k in range(2):
        for way in range(2):
            if k == 0:
                w_step(way, 1, 0).start()
            tok_step(way, 1, ends(way, k)).start()
    for c in range(2):
        sib_step(0, c).start()

    own_filt.wait()
    fstage[...] = filt[...].astype(BF16)
    for copy in own_params:
        copy.wait()
    pstage[...] = jnp.zeros_like(pstage)
    for i in range(3):
        for b in range(3):
            pstage[i * 3 + b : i * 3 + b + 1, :] = short[i, b : b + 1, :]
    pstage[9:10, :] = skip[...]

    def f_step(i):
        return remote(
            fstage.at[pl.ds(i * 16, 16)], fmid.at[zl, zh], f_send.at[i], f_recv.at[0],
            filter_holder(i),
        )

    def g_step(delta):
        target = (y + delta) % 8
        return remote(
            fturn.at[target], fbuf.at[y], g_send.at[delta], g_recv.at[0],
            device(target, zh, x, zl, core),
        )

    def p_step(delta):
        mate = (quarter + delta) % 4
        return remote(
            pstage, pbuf, p_send.at[delta], p_recv.at[0], device(y, zh, x, mate // 2, mate % 2)
        )

    for i in range(8):
        @pl.when(jnp.logical_not(at_home & (own_block == i)))
        def _():
            f_step(i).start()

    @pl.when(at_home)
    def _():
        pltpu.make_async_copy(
            fstage.at[pl.ds(pl.multiple_of(own_block * 16, 16), 16)], fmid.at[zl, zh],
            f_recv.at[0],
        ).start()

    @pl.when(mirrored)
    def _():
        pltpu.make_async_copy(pstage, pbuf, p_recv.at[0]).start()
        for delta in range(1, 4):
            p_step(delta).start()

    for k in range(1, 4):
        wa_step(k).wait_recv()
        for way in range(2):
            w_step(way, 1, k).start()

    def pass_tokens(d, k):
        for way in range(2):
            c = ends(way, k)
            tok_step(way, d, c).wait_recv()
            if d < 4 and goes(d + 1, way, k):
                tok_step(way, d + 1, c).start()
            sib_step(d if way == 0 else 8 - d, c).start()

    def pass_weights(d, k):
        for way in range(2):
            if d < 4 or k // 2 == way:
                w_step(way, d, k).wait_recv()
                if d < 3 or (d == 3 and k // 2 == way):
                    w_step(way, d + 1, k).start()

    def await_sibling(d):
        for half in range(2):
            for way in range(2):
                if (0 < d < 4) or (d == 0 and way == 0) or (d == 4 and half == way):
                    sib_step(0 if d == 0 else (d if way == 0 else 8 - d), half).wait_recv()

    sign = 2 * zl - 1
    blocks = [zh, (zh + sign) % 4, (zh - sign) % 4, (zh + 2) % 4]
    near = [[0], [1, 7], [2, 6], [3, 5], [4]]

    def x_step(p, row):
        return remote(
            sbuf.at[p, row], rbuf.at[p, x, row % 2], x_send.at[p, row], x_recv.at[p],
            device(y, zh, row // 2, zl, core),
        )

    def project(p, steps):
        rows = [(y + delta) % 8 for step in steps for delta in near[step]]
        total = jnp.zeros((48 * len(rows), 256), F32)
        for half in range(2):
            for side in range(2):
                left = jnp.concatenate([wbuf[row, half * 2 + side].reshape(48, 512) for row in rows], 0)
                right = tok[blocks[p] * 2 + half, side].reshape(256, 512)
                total = total + lax.dot_general(
                    left, right, (((1,), (1,)), ((), ())), preferred_element_type=F32
                )
        rounded = total.astype(BF16)
        for n, row in enumerate(rows):
            sbuf[p, row] = rounded[n * 48 : (n + 1) * 48, :]
        for row in rows:
            @pl.when(row // 2 != x)
            def _():
                x_step(p, row).start()

            @pl.when(row // 2 == x)
            def _():
                pltpu.make_async_copy(
                    sbuf.at[p, row], rbuf.at[p, x, row % 2], x_recv.at[p]
                ).start()

    def sum_over_x(p):
        pltpu.make_async_copy(rbuf.at[p], rbuf.at[p], x_recv.at[p]).wait()
        total = rbuf[p, 0].astype(F32)
        for n in range(1, 4):
            total = total + rbuf[p, n].astype(F32)
        total = total.reshape(96, 256)
        for j in range(2):
            sums[p, pl.ds(j, 96, stride=2), :] = total[:, j * 128 : (j + 1) * 128]

    def pieces(p, target):
        first_row = (target // 4) * 96 + (target % 4) * 8
        return [sums[p, first_row + b * 32 : first_row + b * 32 + 8, :] for b in range(3)]

    def e_step(delta):
        target = (y + delta) % 8
        return remote(
            aearly.at[target], xearly.at[y], e_send.at[delta], e_recv.at[0],
            device(target, zh, x, zl, core),
        )

    def a_step(delta):
        target = (y + delta) % 8
        return remote(
            alate.at[target], xlate.at[y], a_send.at[delta], a_recv.at[0],
            device(target, zh, x, zl, core),
        )

    padding = jnp.zeros((8, 128), F32)

    def reduce_early():
        for p in range(3):
            sum_over_x(p)
        for target in range(8):
            parts = pieces(0, target) + pieces(1, target) + pieces(2, target)
            aearly[target] = jnp.concatenate(parts + [padding], 0).astype(BF16)
        for delta in range(1, 8):
            e_step(delta).start()
        pltpu.make_async_copy(aearly.at[y], xearly.at[y], e_recv.at[0]).start()

    def reduce_late():
        sum_over_x(3)
        for target in range(8):
            alate[target] = jnp.concatenate(pieces(3, target) + [padding], 0).astype(BF16)
        for delta in range(1, 8):
            a_step(delta).start()
        pltpu.make_async_copy(alate.at[y], xlate.at[y], a_recv.at[0]).start()

    def transform(value):
        stage = table_left(first[...], value)
        rows = []
        for ch in range(4):
            re = stage[:64, ch * 128 : (ch + 1) * 128]
            im = stage[64:, ch * 128 : (ch + 1) * 128]
            rows.append(
                jnp.concatenate(
                    [re * twist[0] + im * twist[1], im * twist[0] - re * twist[1]], 1
                )
            )
        return table_right(jnp.concatenate(rows, 0), second[...])

    pass_weights(1, 0)
    pass_tokens(1, 0)
    pass_weights(1, 1)
    pass_tokens(1, 1)
    pass_weights(1, 2)
    pass_weights(1, 3)
    await_sibling(0)
    await_sibling(1)
    pass_weights(2, 0)
    pass_tokens(2, 0)
    pass_weights(2, 1)
    project(0, [0, 1])
    pass_tokens(2, 1)
    pass_weights(2, 2)
    pass_weights(2, 3)

    pltpu.make_async_copy(fmid, fmid, f_recv.at[0]).wait()
    for side in range(2):
        for from_zh in range(4):
            piece = fmid[side, from_zh].astype(F32)
            for j in range(2):
                fwide[pl.ds(side * 128 + from_zh * 2 + j, 16, stride=8), :] = piece[
                    :, j * 128 : (j + 1) * 128
                ]
    fturn[...] = fwide[...].astype(BF16).reshape(8, 32, 128)
    for delta in range(1, 8):
        g_step(delta).start()
    pltpu.make_async_copy(fturn.at[y], fbuf.at[y], g_recv.at[0]).start()

    await_sibling(2)
    pass_weights(3, 0)
    pass_tokens(3, 0)
    pass_weights(3, 1)
    project(0, [2])
    project(1, [0, 1, 2])
    pass_tokens(3, 1)
    pass_weights(3, 2)
    pass_weights(3, 3)
    await_sibling(3)
    project(2, [0, 1, 2, 3])
    project(0, [3])
    project(1, [3])

    pltpu.make_async_copy(fbuf, fbuf, g_recv.at[0]).wait()
    pltpu.make_async_copy(pbuf, pbuf, p_recv.at[0]).wait()
    for copy in own_tables:
        copy.wait()
    fwide[...] = fbuf[...].astype(F32).reshape(256, 128)
    lanes = []
    for ch in range(4):
        lanes.append(
            jnp.concatenate(
                [fwide[pl.ds(ch * 8 + inner, 8, stride=32), :] for inner in range(8)], 0
            )
        )
    spectrum[...] = transform(jnp.concatenate(lanes, 1)) * (1.0 / 8192.0)

    for k in range(4):
        pass_weights(4, k)
    project(0, [4])
    project(1, [4])
    project(2, [4])
    pass_tokens(4, 0)
    await_sibling(4)
    project(3, [0, 1, 2, 3, 4])
    reduce_early()
    reduce_late()

    channel = 64 * (zh % 2) + 32 * zl + 16 * core + 4 * (y % 4)
    lane_at = lax.broadcasted_iota(jnp.int32, (16, 128), 1)
    gains = [
        jnp.sum(jnp.where(lane_at == channel + ch, pbuf[...], 0.0), axis=1, keepdims=True)
        for ch in range(4)
    ]
    pltpu.make_async_copy(xearly, xearly, e_recv.at[0]).wait()
    early = xearly[...].astype(F32)
    for p in range(3):
        xwide[blocks[p]] = early[:, p * 24 : (p + 1) * 24, :].reshape(192, 128)
    pltpu.make_async_copy(xlate, xlate, a_recv.at[0]).wait()
    xwide[blocks[3]] = xlate[...].astype(F32)[:, :24, :].reshape(192, 128)
    lane = lax.broadcasted_iota(jnp.int32, (64, 128), 1)
    below = lax.broadcasted_iota(jnp.int32, (8, 128), 0)

    def mixed(b, ch):
        here = jnp.concatenate(
            [
                xwide[inner // 2, pl.ds((b * 4 + ch) * 2 + inner % 2, 8, stride=24), :]
                for inner in range(8)
            ],
            0,
        )
        total = gains[ch][b : b + 1, :] * here
        for i in range(1, 3):
            turned = pltpu.roll(here, i, 1)
            wrapped = jnp.where(below == 0, 0.0, pltpu.roll(turned[56:, :], 1, 0))
            before = jnp.concatenate([wrapped, turned[:56, :]], 0)
            total = total + gains[ch][i * 3 + b : i * 3 + b + 1, :] * jnp.where(
                lane < i, before, turned
            )
        return total

    drives = [mixed(1, ch) * mixed(2, ch) for ch in range(4)]
    wave = transform(jnp.concatenate(drives, 1))
    wave_re, wave_im = wave[:, :128], wave[:, 128:]
    filt_re, filt_im = spectrum[:, :128], spectrum[:, 128:]
    product = jnp.concatenate(
        [wave_re * filt_re - wave_im * filt_im, wave_re * filt_im + wave_im * filt_re], 1
    )
    back = table_right(product, jnp.transpose(second[...], (1, 0)))
    columns = []
    for ch in range(4):
        re = back[ch * 64 : (ch + 1) * 64, :128]
        im = back[ch * 64 : (ch + 1) * 64, 128:]
        columns.append(
            jnp.concatenate(
                [re * twist[0] - im * twist[1], im * twist[0] + re * twist[1]], 0
            )
        )
    convolved = table_left(last[...], jnp.concatenate(columns, 1))
    for ch in range(4):
        gated = mixed(0, ch) * (
            convolved[:, ch * 128 : (ch + 1) * 128] + gains[ch][9:10, :] * drives[ch]
        )
        for inner in range(8):
            fwide[pl.ds(ch * 8 + inner, 8, stride=32), :] = gated[
                inner * 8 : (inner + 1) * 8, :
            ]

    oturn[...] = fwide[...].astype(BF16).reshape(8, 32, 128)

    def n_step(delta):
        target = (y + delta) % 8
        return remote(
            oturn.at[target], omid.at[y], n_send.at[delta], n_recv.at[0],
            device(target, zh, x, zl, core),
        )

    for delta in range(1, 8):
        n_step(delta).start()
    pltpu.make_async_copy(oturn.at[y], omid.at[y], n_recv.at[0]).start()

    out_rows = out.at[pl.ds(pl.multiple_of(own_block * 16, 16), 16)]

    def o_step(i):
        return remote(ostage.at[i], out_rows, o_send.at[i], o_recv.at[0], out_owner(i))

    pltpu.make_async_copy(omid, omid, n_recv.at[0]).wait()
    fwide[...] = omid[...].astype(F32).reshape(256, 128)
    for i in range(8):
        first_row = (i // 4) * 128 + (i % 4) * 2
        ostage[i] = jnp.concatenate(
            [fwide[pl.ds(first_row + j, 16, stride=8), :] for j in range(2)], 1
        ).astype(BF16)
    for i in range(8):
        @pl.when(jnp.logical_not(at_home & (own_out == i)))
        def _():
            o_step(i).start()

    @pl.when(at_home)
    def _():
        pltpu.make_async_copy(ostage.at[own_out], out_rows, o_recv.at[0]).start()

    for d in range(1, 5):
        for k in range(4):
            for way in range(2):
                if k < 2 and goes(d, way, k):
                    tok_step(way, d, ends(way, k)).wait_send()
                if d < 4 or k // 2 == way:
                    w_step(way, d, k).wait_send()
    for slot in range(8):
        for half in range(2):
            sib_step(slot, half).wait_send()
    for k in range(1, 4):
        wa_step(k).wait_send()
    for p in range(4):
        for row in range(8):
            @pl.when(row // 2 != x)
            def _():
                x_step(p, row).wait_send()

    @pl.when(mirrored)
    def _():
        for delta in range(1, 4):
            p_step(delta).wait_send()

    for i in range(8):
        @pl.when(jnp.logical_not(at_home & (own_block == i)))
        def _():
            f_step(i).wait_send()

        @pl.when(jnp.logical_not(at_home & (own_out == i)))
        def _():
            o_step(i).wait_send()

    for delta in range(1, 8):
        g_step(delta).wait_send()
        e_step(delta).wait_send()
        a_step(delta).wait_send()
        n_step(delta).wait_send()
    pltpu.make_async_copy(out, out, o_recv.at[0]).wait()


def per_device(tokens, in_weight, short_filter, long_filter, skip_gain):
    consts = [jnp.asarray(table) for table in tables()]
    dma = pltpu.SemaphoreType.DMA
    hbm = pl.BlockSpec(memory_space=pltpu.HBM)
    columns = jnp.transpose(in_weight, (0, 2, 1)).reshape(3, 4, 16, 512)
    return pl.pallas_call(
        kernel,
        out_shape=jax.ShapeDtypeStruct((128, 256), BF16),
        in_specs=[hbm] * 9,
        out_specs=hbm,
        scratch_shapes=[
            pltpu.VMEM((128, 64), F32),
            pltpu.VMEM((2, 64, 128), F32),
            pltpu.VMEM((256, 256), F32),
            pltpu.VMEM((64, 128), F32),
            pltpu.VMEM((3, 3, 128), F32),
            pltpu.VMEM((1, 128), F32),
            pltpu.VMEM((128, 256), F32),
            pltpu.VMEM((8, 2, 2, 128, 512), BF16),
            pltpu.VMEM((3, 4, 16, 512), BF16),
            pltpu.VMEM((8, 4, 3, 16, 512), BF16),
            pltpu.VMEM((4, 8, 48, 256), BF16),
            pltpu.VMEM((4, 4, 2, 48, 256), BF16),
            pltpu.VMEM((4, 192, 128), F32),
            pltpu.VMEM((8, 80, 128), BF16),
            pltpu.VMEM((8, 80, 128), BF16),
            pltpu.VMEM((8, 32, 128), BF16),
            pltpu.VMEM((8, 32, 128), BF16),
            pltpu.VMEM((4, 192, 128), F32),
            pltpu.VMEM((128, 256), BF16),
            pltpu.VMEM((2, 4, 16, 256), BF16),
            pltpu.VMEM((256, 128), F32),
            pltpu.VMEM((8, 32, 128), BF16),
            pltpu.VMEM((8, 32, 128), BF16),
            pltpu.VMEM((16, 128), F32),
            pltpu.VMEM((16, 128), F32),
            pltpu.VMEM((256, 256), F32),
            pltpu.VMEM((8, 32, 128), BF16),
            pltpu.VMEM((8, 32, 128), BF16),
            pltpu.VMEM((8, 16, 256), BF16),
            dma((1,)), dma((1,)), dma((1,)), dma((2,)), dma((4,)),
            dma((2, 4, 2)), dma((2, 4, 2)),
            dma((8, 2)), dma((8, 2)),
            dma((4,)), dma((4,)),
            dma((2, 4, 4)), dma((2, 4, 4)),
            dma((4, 8)), dma((4,)),
            dma((8,)), dma((1,)),
            dma((8,)), dma((1,)),
            dma((8,)), dma((1,)),
            dma((8,)), dma((1,)),
            dma((4,)), dma((1,)),
            dma((8,)), dma((1,)),
            dma((8,)), dma((1,)),
        ],
        compiler_params=pltpu.CompilerParams(
            collective_id=0, has_side_effects=True, vmem_limit_bytes=63 * 1024 * 1024
        ),
    )(tokens.reshape(2, 128, 512), columns, short_filter, long_filter, skip_gain[None, :], *consts)


def solution(mesh):
    placed = (
        P("seq", "chan"),
        P(None, "chan", "seq"),
        P(None, None, "chan"),
        P("chan", "seq"),
        P("chan"),
    )
    return jax.shard_map(
        per_device, mesh=mesh, in_specs=placed, out_specs=P("chan", "seq"), check_vma=False
    )
```

```python
import jax
import jax.numpy as jnp
import numpy as np
from jax import lax
from jax.experimental import pallas as pl
from jax.experimental.pallas import tpu as pltpu
from jax.sharding import PartitionSpec as P

MESH = pl.DeviceIdType.MESH
F32 = jnp.float32
BF16 = jnp.bfloat16


def tables():
    row = np.arange(64)
    outer = 8 * (row % 8) + row // 8
    freq = np.arange(64) + 0.25
    lane = np.arange(128)
    chi = 2 * np.pi * np.outer(freq, outer) / 64
    phi = 2 * np.pi * np.outer(freq, lane) / 8192
    psi = 2 * np.pi * np.outer(lane, lane) / 128
    first = np.concatenate([np.cos(chi), -np.sin(chi)], 0)
    twist = np.stack([np.cos(phi), np.sin(phi)]).astype(np.float32)
    second = np.block([[np.cos(psi), -np.sin(psi)], [np.sin(psi), np.cos(psi)]])
    last = np.concatenate([np.cos(chi).T, -np.sin(chi).T], 1)
    return (
        first.astype(np.float32),
        twist,
        second.astype(np.float32),
        last.astype(np.float32),
    )


def split(value):
    high = value.astype(BF16)
    return high, (value - high.astype(F32)).astype(BF16)


def dot(left, right):
    return jnp.dot(left, right, preferred_element_type=F32)


def table_left(table, value):
    table = split(table)
    high, low = split(value)
    return dot(table[0], high) + (dot(table[0], low) + dot(table[1], high))


def table_right(value, table):
    table = split(table)
    high, low = split(value)
    return dot(high, table[0]) + (dot(low, table[0]) + dot(high, table[1]))


def kernel(
    tok_in, w_in, short_in, filt_in, skip_in, first_in, twist_in, second_in, last_in,
    out,
    first, twist, second, last, short, skip, filt,
    tok, wown, wbuf, sbuf, rbuf, sums, aearly, xearly, alate, xlate, xwide,
    fstage, fmid, fwide, fturn, fbuf, pstage, pbuf, spectrum, oturn, omid, ostage,
    in_sem, tok_sem, own_sem, param_sem, table_sem,
    tok_send, tok_recv, sib_send, sib_recv, wa_send, wa_recv, wr_send, wr_recv,
    x_send, x_recv, e_send, e_recv, a_send, a_recv, f_send, f_recv, g_send, g_recv, p_send, p_recv,
    n_send, n_recv, o_send, o_recv,
):
    seq, chan = lax.axis_index("seq"), lax.axis_index("chan")
    y, zh = seq // 4, seq % 4
    x, zl, core = chan // 4, (chan // 2) % 2, chan % 2
    z = zh * 2 + zl

    def device(y_, zh_, x_, zl_, core_):
        return (y_ * 4 + zh_, (x_ * 2 + zl_) * 2 + core_)

    def device_z(z_):
        return device(y, z_ // 2, x, z_ % 2, core)

    sibling = device(y, zh, x, zl, 1 - core)
    mirrored = (zl == y // 4) & (core == zh // 2)

    def filter_holder(i):
        return device(y, 2 * core + i // 4, x, (i // 2) % 2, i % 2)

    def out_owner(i):
        return device(y, i % 4, x, i // 4, zh // 2)

    at_home = core == zh // 2
    own_block = (zh % 2) * 4 + zl * 2 + core
    own_out = zl * 4 + zh

    barrier = pltpu.get_barrier_semaphore()

    def greet(target):
        pl.semaphore_signal(barrier, inc=1, device_id=target, device_id_type=MESH)

    greet(device_z((z + 1) % 8))
    greet(device_z((z + 7) % 8))
    greet(device((y + 1) % 8, zh, x, zl, core))
    greet(device((y + 7) % 8, zh, x, zl, core))
    for delta in range(1, 4):
        mate = (zl * 2 + core + delta) % 4
        greet(device(y, zh, x, mate // 2, mate % 2))
        greet(device(y, zh, (x + delta) % 4, zl, core))

    quarter = zl * 2 + core
    own_tok = pltpu.make_async_copy(tok_in, tok.at[z, core], tok_sem.at[0])
    own_w = pltpu.make_async_copy(w_in, wown, own_sem.at[0])
    own_filt = pltpu.make_async_copy(filt_in, filt, in_sem.at[0])
    own_params = [
        pltpu.make_async_copy(short_in, short, param_sem.at[0]),
        pltpu.make_async_copy(skip_in, skip, param_sem.at[1]),
    ]
    own_tables = [
        pltpu.make_async_copy(first_in, first, table_sem.at[0]),
        pltpu.make_async_copy(twist_in, twist, table_sem.at[1]),
        pltpu.make_async_copy(second_in, second, table_sem.at[2]),
        pltpu.make_async_copy(last_in, last, table_sem.at[3]),
    ]
    for copy in [own_tok, own_w, own_filt] + own_params + own_tables:
        copy.start()

    pl.semaphore_wait(barrier, 10)

    def remote(src, dst, send, recv, target):
        return pltpu.make_async_remote_copy(
            src_ref=src, dst_ref=dst, send_sem=send, recv_sem=recv,
            device_id=target, device_id_type=MESH,
        )

    def tok_step(way, d, c):
        shard = (z - (d - 1)) % 8 if way == 0 else (z + (d - 1)) % 8
        target = device_z((z + 1) % 8 if way == 0 else (z + 7) % 8)
        ref = tok.at[shard, core, c]
        return remote(
            ref, ref, tok_send.at[way, d - 1, c], tok_recv.at[way, d - 1, c], target
        )

    def sib_step(slot, c):
        ref = tok.at[(z - slot) % 8, core, c]
        return remote(ref, ref, sib_send.at[slot, c], sib_recv.at[slot, c], sibling)

    def w_step(way, d, k):
        shard = (y - (d - 1)) % 8 if way == 0 else (y + (d - 1)) % 8
        target = device((y + 1) % 8 if way == 0 else (y + 7) % 8, zh, x, zl, core)
        ref = wbuf.at[shard, held(k)]
        return remote(
            ref, ref, wr_send.at[way, d - 1, k], wr_recv.at[way, d - 1, k], target
        )

    def held(k):
        flipped = core if k % 2 == 0 else 1 - core
        return (zl if k < 2 else 1 - zl) * 2 + flipped

    def goes(d, way, k):
        return d < 4 or k < 1

    def wa_step(k):
        mate = held(k)
        return remote(
            wown.at[:, mate], wbuf.at[y, quarter], wa_send.at[k], wa_recv.at[k],
            device(y, zh, x, mate // 2, mate % 2),
        )

    def ends(way, k):
        return k if way == 0 else 1 - k

    own_w.wait()
    for k in range(1, 4):
        wa_step(k).start()
    wbuf[y, quarter] = wown[:, quarter]
    own_tok.wait()
    for k in range(2):
        for way in range(2):
            if k == 0:
                w_step(way, 1, 0).start()
            tok_step(way, 1, ends(way, k)).start()
    for c in range(2):
        sib_step(0, c).start()

    own_filt.wait()
    fstage[...] = filt[...].astype(BF16)
    for copy in own_params:
        copy.wait()
    pstage[...] = jnp.zeros_like(pstage)
    for i in range(3):
        for b in range(3):
            pstage[i * 3 + b : i * 3 + b + 1, :] = short[i, b : b + 1, :]
    pstage[9:10, :] = skip[...]

    def f_step(i):
        return remote(
            fstage.at[pl.ds(i * 16, 16)], fmid.at[zl, zh], f_send.at[i], f_recv.at[0],
            filter_holder(i),
        )

    def g_step(delta):
        target = (y + delta) % 8
        return remote(
            fturn.at[target], fbuf.at[y], g_send.at[delta], g_recv.at[0],
            device(target, zh, x, zl, core),
        )

    def p_step(delta):
        mate = (quarter + delta) % 4
        return remote(
            pstage, pbuf, p_send.at[delta], p_recv.at[0], device(y, zh, x, mate // 2, mate % 2)
        )

    @pl.when(mirrored)
    def _():
        pltpu.make_async_copy(pstage, pbuf, p_recv.at[0]).start()
        for delta in range(1, 4):
            p_step(delta).start()

    for k in range(1, 4):
        wa_step(k).wait_recv()
        for way in range(2):
            w_step(way, 1, k).start()

    def pass_tokens(d, k):
        for way in range(2):
            c = ends(way, k)
            tok_step(way, d, c).wait_recv()
            if d < 4 and goes(d + 1, way, k):
                tok_step(way, d + 1, c).start()
            sib_step(d if way == 0 else 8 - d, c).start()

    def pass_weights(d, k):
        for way in range(2):
            if d < 4 or k // 2 == way:
                w_step(way, d, k).wait_recv()
                if d < 3 or (d == 3 and k // 2 == way):
                    w_step(way, d + 1, k).start()

    def await_sibling(d):
        for half in range(2):
            for way in range(2):
                if (0 < d < 4) or (d == 0 and way == 0) or (d == 4 and half == way):
                    sib_step(0 if d == 0 else (d if way == 0 else 8 - d), half).wait_recv()

    sign = 2 * zl - 1
    blocks = [zh, (zh + sign) % 4, (zh - sign) % 4, (zh + 2) % 4]
    near = [[0], [1, 7], [2, 6], [3, 5], [4]]

    def x_step(p, row):
        return remote(
            sbuf.at[p, row], rbuf.at[p, x, row % 2], x_send.at[p, row], x_recv.at[p],
            device(y, zh, row // 2, zl, core),
        )

    def project(p, steps):
        rows = [(y + delta) % 8 for step in steps for delta in near[step]]
        total = jnp.zeros((48 * len(rows), 256), F32)
        for half in range(2):
            for side in range(2):
                left = jnp.concatenate([wbuf[row, half * 2 + side].reshape(48, 512) for row in rows], 0)
                right = tok[blocks[p] * 2 + half, side].reshape(256, 512)
                total = total + lax.dot_general(
                    left, right, (((1,), (1,)), ((), ())), preferred_element_type=F32
                )
        rounded = total.astype(BF16)
        for n, row in enumerate(rows):
            sbuf[p, row] = rounded[n * 48 : (n + 1) * 48, :]
        for row in rows:
            @pl.when(row // 2 != x)
            def _():
                x_step(p, row).start()

            @pl.when(row // 2 == x)
            def _():
                pltpu.make_async_copy(
                    sbuf.at[p, row], rbuf.at[p, x, row % 2], x_recv.at[p]
                ).start()

    def sum_over_x(p):
        pltpu.make_async_copy(rbuf.at[p], rbuf.at[p], x_recv.at[p]).wait()
        total = rbuf[p, 0].astype(F32)
        for n in range(1, 4):
            total = total + rbuf[p, n].astype(F32)
        total = total.reshape(96, 256)
        for j in range(2):
            sums[p, pl.ds(j, 96, stride=2), :] = total[:, j * 128 : (j + 1) * 128]

    def pieces(p, target):
        first_row = (target // 4) * 96 + (target % 4) * 8
        return [sums[p, first_row + b * 32 : first_row + b * 32 + 8, :] for b in range(3)]

    def e_step(delta):
        target = (y + delta) % 8
        return remote(
            aearly.at[target], xearly.at[y], e_send.at[delta], e_recv.at[0],
            device(target, zh, x, zl, core),
        )

    def a_step(delta):
        target = (y + delta) % 8
        return remote(
            alate.at[target], xlate.at[y], a_send.at[delta], a_recv.at[0],
            device(target, zh, x, zl, core),
        )

    padding = jnp.zeros((8, 128), F32)

    def reduce_early():
        for p in range(3):
            sum_over_x(p)
        for target in range(8):
            parts = pieces(0, target) + pieces(1, target) + pieces(2, target)
            aearly[target] = jnp.concatenate(parts + [padding], 0).astype(BF16)
        for delta in range(1, 8):
            e_step(delta).start()
        pltpu.make_async_copy(aearly.at[y], xearly.at[y], e_recv.at[0]).start()

    def reduce_late():
        sum_over_x(3)
        for target in range(8):
            alate[target] = jnp.concatenate(pieces(3, target) + [padding], 0).astype(BF16)
        for delta in range(1, 8):
            a_step(delta).start()
        pltpu.make_async_copy(alate.at[y], xlate.at[y], a_recv.at[0]).start()

    def transform(value):
        stage = table_left(first[...], value)
        rows = []
        for ch in range(4):
            re = stage[:64, ch * 128 : (ch + 1) * 128]
            im = stage[64:, ch * 128 : (ch + 1) * 128]
            rows.append(
                jnp.concatenate(
                    [re * twist[0] + im * twist[1], im * twist[0] - re * twist[1]], 1
                )
            )
        return table_right(jnp.concatenate(rows, 0), second[...])

    pass_weights(1, 0)
    pass_tokens(1, 0)
    pass_weights(1, 1)
    pass_tokens(1, 1)
    pass_weights(1, 2)
    pass_weights(1, 3)
    await_sibling(0)
    await_sibling(1)
    pass_weights(2, 0)
    pass_tokens(2, 0)
    pass_weights(2, 1)
    project(0, [0, 1])
    pass_tokens(2, 1)
    pass_weights(2, 2)
    pass_weights(2, 3)

    await_sibling(2)
    pass_weights(3, 0)
    pass_tokens(3, 0)
    pass_weights(3, 1)
    project(0, [2])
    project(1, [0, 1, 2])
    pass_tokens(3, 1)
    pass_weights(3, 2)
    pass_weights(3, 3)
    await_sibling(3)
    project(2, [0, 1, 2, 3])
    project(0, [3])
    project(1, [3])

    for k in range(4):
        pass_weights(4, k)
    project(0, [4])
    project(1, [4])
    project(2, [4])
    pass_tokens(4, 0)
    await_sibling(4)
    for i in range(8):
        @pl.when(jnp.logical_not(at_home & (own_block == i)))
        def _():
            f_step(i).start()

    @pl.when(at_home)
    def _():
        pltpu.make_async_copy(
            fstage.at[pl.ds(pl.multiple_of(own_block * 16, 16), 16)], fmid.at[zl, zh],
            f_recv.at[0],
        ).start()

    project(3, [0, 1, 2, 3, 4])
    reduce_early()

    pltpu.make_async_copy(fmid, fmid, f_recv.at[0]).wait()
    for side in range(2):
        for from_zh in range(4):
            piece = fmid[side, from_zh].astype(F32)
            for j in range(2):
                fwide[pl.ds(side * 128 + from_zh * 2 + j, 16, stride=8), :] = piece[
                    :, j * 128 : (j + 1) * 128
                ]
    fturn[...] = fwide[...].astype(BF16).reshape(8, 32, 128)
    for delta in range(1, 8):
        g_step(delta).start()
    pltpu.make_async_copy(fturn.at[y], fbuf.at[y], g_recv.at[0]).start()

    reduce_late()

    pltpu.make_async_copy(fbuf, fbuf, g_recv.at[0]).wait()
    pltpu.make_async_copy(pbuf, pbuf, p_recv.at[0]).wait()
    for copy in own_tables:
        copy.wait()
    fwide[...] = fbuf[...].astype(F32).reshape(256, 128)
    lanes = []
    for ch in range(4):
        lanes.append(
            jnp.concatenate(
                [fwide[pl.ds(ch * 8 + inner, 8, stride=32), :] for inner in range(8)], 0
            )
        )
    spectrum[...] = transform(jnp.concatenate(lanes, 1)) * (1.0 / 8192.0)

    channel = 64 * (zh % 2) + 32 * zl + 16 * core + 4 * (y % 4)
    lane_at = lax.broadcasted_iota(jnp.int32, (16, 128), 1)
    gains = [
        jnp.sum(jnp.where(lane_at == channel + ch, pbuf[...], 0.0), axis=1, keepdims=True)
        for ch in range(4)
    ]
    pltpu.make_async_copy(xearly, xearly, e_recv.at[0]).wait()
    early = xearly[...].astype(F32)
    for p in range(3):
        xwide[blocks[p]] = early[:, p * 24 : (p + 1) * 24, :].reshape(192, 128)
    pltpu.make_async_copy(xlate, xlate, a_recv.at[0]).wait()
    xwide[blocks[3]] = xlate[...].astype(F32)[:, :24, :].reshape(192, 128)
    lane = lax.broadcasted_iota(jnp.int32, (64, 128), 1)
    below = lax.broadcasted_iota(jnp.int32, (8, 128), 0)

    def mixed(b, ch):
        here = jnp.concatenate(
            [
                xwide[inner // 2, pl.ds((b * 4 + ch) * 2 + inner % 2, 8, stride=24), :]
                for inner in range(8)
            ],
            0,
        )
        total = gains[ch][b : b + 1, :] * here
        for i in range(1, 3):
            turned = pltpu.roll(here, i, 1)
            wrapped = jnp.where(below == 0, 0.0, pltpu.roll(turned[56:, :], 1, 0))
            before = jnp.concatenate([wrapped, turned[:56, :]], 0)
            total = total + gains[ch][i * 3 + b : i * 3 + b + 1, :] * jnp.where(
                lane < i, before, turned
            )
        return total

    drives = [mixed(1, ch) * mixed(2, ch) for ch in range(4)]
    wave = transform(jnp.concatenate(drives, 1))
    wave_re, wave_im = wave[:, :128], wave[:, 128:]
    filt_re, filt_im = spectrum[:, :128], spectrum[:, 128:]
    product = jnp.concatenate(
        [wave_re * filt_re - wave_im * filt_im, wave_re * filt_im + wave_im * filt_re], 1
    )
    back = table_right(product, jnp.transpose(second[...], (1, 0)))
    columns = []
    for ch in range(4):
        re = back[ch * 64 : (ch + 1) * 64, :128]
        im = back[ch * 64 : (ch + 1) * 64, 128:]
        columns.append(
            jnp.concatenate(
                [re * twist[0] - im * twist[1], im * twist[0] + re * twist[1]], 0
            )
        )
    convolved = table_left(last[...], jnp.concatenate(columns, 1))
    for ch in range(4):
        gated = mixed(0, ch) * (
            convolved[:, ch * 128 : (ch + 1) * 128] + gains[ch][9:10, :] * drives[ch]
        )
        for inner in range(8):
            fwide[pl.ds(ch * 8 + inner, 8, stride=32), :] = gated[
                inner * 8 : (inner + 1) * 8, :
            ]

    oturn[...] = fwide[...].astype(BF16).reshape(8, 32, 128)

    def n_step(delta):
        target = (y + delta) % 8
        return remote(
            oturn.at[target], omid.at[y], n_send.at[delta], n_recv.at[0],
            device(target, zh, x, zl, core),
        )

    for delta in range(1, 8):
        n_step(delta).start()
    pltpu.make_async_copy(oturn.at[y], omid.at[y], n_recv.at[0]).start()

    out_rows = out.at[pl.ds(pl.multiple_of(own_block * 16, 16), 16)]

    def o_step(i):
        return remote(ostage.at[i], out_rows, o_send.at[i], o_recv.at[0], out_owner(i))

    pltpu.make_async_copy(omid, omid, n_recv.at[0]).wait()
    fwide[...] = omid[...].astype(F32).reshape(256, 128)
    for i in range(8):
        first_row = (i // 4) * 128 + (i % 4) * 2
        ostage[i] = jnp.concatenate(
            [fwide[pl.ds(first_row + j, 16, stride=8), :] for j in range(2)], 1
        ).astype(BF16)
    for i in range(8):
        @pl.when(jnp.logical_not(at_home & (own_out == i)))
        def _():
            o_step(i).start()

    @pl.when(at_home)
    def _():
        pltpu.make_async_copy(ostage.at[own_out], out_rows, o_recv.at[0]).start()

    for d in range(1, 5):
        for k in range(4):
            for way in range(2):
                if k < 2 and goes(d, way, k):
                    tok_step(way, d, ends(way, k)).wait_send()
                if d < 4 or k // 2 == way:
                    w_step(way, d, k).wait_send()
    for slot in range(8):
        for half in range(2):
            sib_step(slot, half).wait_send()
    for k in range(1, 4):
        wa_step(k).wait_send()
    for p in range(4):
        for row in range(8):
            @pl.when(row // 2 != x)
            def _():
                x_step(p, row).wait_send()

    @pl.when(mirrored)
    def _():
        for delta in range(1, 4):
            p_step(delta).wait_send()

    for i in range(8):
        @pl.when(jnp.logical_not(at_home & (own_block == i)))
        def _():
            f_step(i).wait_send()

        @pl.when(jnp.logical_not(at_home & (own_out == i)))
        def _():
            o_step(i).wait_send()

    for delta in range(1, 8):
        g_step(delta).wait_send()
        e_step(delta).wait_send()
        a_step(delta).wait_send()
        n_step(delta).wait_send()
    pltpu.make_async_copy(out, out, o_recv.at[0]).wait()


def per_device(tokens, in_weight, short_filter, long_filter, skip_gain):
    consts = [jnp.asarray(table) for table in tables()]
    dma = pltpu.SemaphoreType.DMA
    hbm = pl.BlockSpec(memory_space=pltpu.HBM)
    columns = jnp.transpose(in_weight, (0, 2, 1)).reshape(3, 4, 16, 512)
    return pl.pallas_call(
        kernel,
        out_shape=jax.ShapeDtypeStruct((128, 256), BF16),
        in_specs=[hbm] * 9,
        out_specs=hbm,
        scratch_shapes=[
            pltpu.VMEM((128, 64), F32),
            pltpu.VMEM((2, 64, 128), F32),
            pltpu.VMEM((256, 256), F32),
            pltpu.VMEM((64, 128), F32),
            pltpu.VMEM((3, 3, 128), F32),
            pltpu.VMEM((1, 128), F32),
            pltpu.VMEM((128, 256), F32),
            pltpu.VMEM((8, 2, 2, 128, 512), BF16),
            pltpu.VMEM((3, 4, 16, 512), BF16),
            pltpu.VMEM((8, 4, 3, 16, 512), BF16),
            pltpu.VMEM((4, 8, 48, 256), BF16),
            pltpu.VMEM((4, 4, 2, 48, 256), BF16),
            pltpu.VMEM((4, 192, 128), F32),
            pltpu.VMEM((8, 80, 128), BF16),
            pltpu.VMEM((8, 80, 128), BF16),
            pltpu.VMEM((8, 32, 128), BF16),
            pltpu.VMEM((8, 32, 128), BF16),
            pltpu.VMEM((4, 192, 128), F32),
            pltpu.VMEM((128, 256), BF16),
            pltpu.VMEM((2, 4, 16, 256), BF16),
            pltpu.VMEM((256, 128), F32),
            pltpu.VMEM((8, 32, 128), BF16),
            pltpu.VMEM((8, 32, 128), BF16),
            pltpu.VMEM((16, 128), F32),
            pltpu.VMEM((16, 128), F32),
            pltpu.VMEM((256, 256), F32),
            pltpu.VMEM((8, 32, 128), BF16),
            pltpu.VMEM((8, 32, 128), BF16),
            pltpu.VMEM((8, 16, 256), BF16),
            dma((1,)), dma((1,)), dma((1,)), dma((2,)), dma((4,)),
            dma((2, 4, 2)), dma((2, 4, 2)),
            dma((8, 2)), dma((8, 2)),
            dma((4,)), dma((4,)),
            dma((2, 4, 4)), dma((2, 4, 4)),
            dma((4, 8)), dma((4,)),
            dma((8,)), dma((1,)),
            dma((8,)), dma((1,)),
            dma((8,)), dma((1,)),
            dma((8,)), dma((1,)),
            dma((4,)), dma((1,)),
            dma((8,)), dma((1,)),
            dma((8,)), dma((1,)),
        ],
        compiler_params=pltpu.CompilerParams(
            collective_id=0, has_side_effects=True, vmem_limit_bytes=63 * 1024 * 1024
        ),
    )(tokens.reshape(2, 128, 512), columns, short_filter, long_filter, skip_gain[None, :], *consts)


def solution(mesh):
    placed = (
        P("seq", "chan"),
        P(None, "chan", "seq"),
        P(None, None, "chan"),
        P("chan", "seq"),
        P("chan"),
    )
    return jax.shard_map(
        per_device, mesh=mesh, in_specs=placed, out_specs=P("chan", "seq"), check_vma=False
    )
```

```python
import jax
import jax.numpy as jnp
import numpy as np
from jax import lax
from jax.experimental import pallas as pl
from jax.experimental.pallas import tpu as pltpu
from jax.sharding import PartitionSpec as P

MESH = pl.DeviceIdType.MESH
F32 = jnp.float32
FAR_FIRST = (4, 3, 5, 2, 6, 1, 7)
BF16 = jnp.bfloat16


def tables():
    row = np.arange(64)
    outer = 8 * (row % 8) + row // 8
    freq = np.arange(64) + 0.25
    lane = np.arange(128)
    chi = 2 * np.pi * np.outer(freq, outer) / 64
    phi = 2 * np.pi * np.outer(freq, lane) / 8192
    psi = 2 * np.pi * np.outer(lane, lane) / 128
    first = np.concatenate([np.cos(chi), -np.sin(chi)], 0)
    twist = np.stack([np.cos(phi), np.sin(phi)]).astype(np.float32)
    second = np.block([[np.cos(psi), -np.sin(psi)], [np.sin(psi), np.cos(psi)]])
    last = np.concatenate([np.cos(chi).T, -np.sin(chi).T], 1)
    return (
        first.astype(np.float32),
        twist,
        second.astype(np.float32),
        last.astype(np.float32),
    )


def split(value):
    high = value.astype(BF16)
    return high, (value - high.astype(F32)).astype(BF16)


def dot(left, right):
    return jnp.dot(left, right, preferred_element_type=F32)


def table_left(table, value):
    table = split(table)
    high, low = split(value)
    return dot(table[0], high) + (dot(table[0], low) + dot(table[1], high))


def table_right(value, table):
    table = split(table)
    high, low = split(value)
    return dot(high, table[0]) + (dot(low, table[0]) + dot(high, table[1]))


def kernel(
    tok_in, w_in, short_in, filt_in, skip_in, first_in, twist_in, second_in, last_in,
    out,
    first, twist, second, last, short, skip, filt,
    tok, wown, wbuf, sbuf, rbuf, sums, aearly, xearly, alate, xlate, xwide,
    fstage, fmid, fwide, fturn, fbuf, pstage, pbuf, spectrum, oturn, omid, ostage,
    in_sem, tok_sem, own_sem, param_sem, table_sem,
    tok_send, tok_recv, sib_send, sib_recv, wa_send, wa_recv, wr_send, wr_recv,
    ws_send, ws_recv,
    x_send, x_recv, e_send, e_recv, a_send, a_recv, f_send, f_recv, g_send, g_recv, p_send, p_recv,
    n_send, n_recv, o_send, o_recv,
):
    seq, chan = lax.axis_index("seq"), lax.axis_index("chan")
    y, zh = seq // 4, seq % 4
    x, zl, core = chan // 4, (chan // 2) % 2, chan % 2
    z = zh * 2 + zl

    def device(y_, zh_, x_, zl_, core_):
        return (y_ * 4 + zh_, (x_ * 2 + zl_) * 2 + core_)

    def device_z(z_):
        return device(y, z_ // 2, x, z_ % 2, core)

    sibling = device(y, zh, x, zl, 1 - core)
    mirrored = (zl == y // 4) & (core == zh // 2)

    def filter_holder(i):
        return device(y, 2 * core + i // 4, x, (i // 2) % 2, i % 2)

    def out_owner(i):
        return device(y, i % 4, x, i // 4, zh // 2)

    at_home = core == zh // 2
    own_block = (zh % 2) * 4 + zl * 2 + core
    own_out = zl * 4 + zh

    barrier = pltpu.get_barrier_semaphore()

    def greet(target):
        pl.semaphore_signal(barrier, inc=1, device_id=target, device_id_type=MESH)

    @pl.when(core == 0)
    def _():
        greet(device_z((z + 1) % 8))
        greet(device_z((z + 7) % 8))

    @pl.when(core == 1)
    def _():
        greet(device((y + 1) % 8, zh, x, zl, core))
        greet(device((y + 7) % 8, zh, x, zl, core))

    for delta in range(1, 4):
        mate = (zl * 2 + core + delta) % 4
        greet(device(y, zh, x, mate // 2, mate % 2))
        greet(device(y, zh, (x + delta) % 4, zl, core))

    quarter = zl * 2 + core
    own_tok = [
        pltpu.make_async_copy(tok_in.at[c], tok.at[z, c, core], tok_sem.at[c]) for c in range(2)
    ]
    own_w = pltpu.make_async_copy(w_in, wown, own_sem.at[0])
    own_filt = pltpu.make_async_copy(filt_in, filt, in_sem.at[0])
    own_params = [
        pltpu.make_async_copy(short_in, short, param_sem.at[0]),
        pltpu.make_async_copy(skip_in, skip, param_sem.at[1]),
    ]
    own_tables = [
        pltpu.make_async_copy(first_in, first, table_sem.at[0]),
        pltpu.make_async_copy(twist_in, twist, table_sem.at[1]),
        pltpu.make_async_copy(second_in, second, table_sem.at[2]),
        pltpu.make_async_copy(last_in, last, table_sem.at[3]),
    ]
    for copy in own_tok + [own_w, own_filt] + own_params + own_tables:
        copy.start()

    pl.semaphore_wait(barrier, 8)

    def remote(src, dst, send, recv, target):
        return pltpu.make_async_remote_copy(
            src_ref=src, dst_ref=dst, send_sem=send, recv_sem=recv,
            device_id=target, device_id_type=MESH,
        )

    def ends(way, k):
        return k // 2 ^ way, k % 2

    def goes(d, way, k):
        return d < 4 or k < 2

    def w_goes(d, way, k):
        return d < 4 or k == way

    def tok_step(way, d, k):
        shard = (z - (d - 1)) % 8 if way == 0 else (z + (d - 1)) % 8
        target = device_z((z + 1) % 8 if way == 0 else (z + 7) % 8)
        part, side = ends(way, k)
        ref = tok.at[shard, part, side]
        return remote(
            ref, ref, tok_send.at[way, d - 1, k], tok_recv.at[way, d - 1, k], target
        )

    def swap_step(part):
        ref = tok.at[z, part, core]
        return remote(ref, ref, sib_send.at[0, part], sib_recv.at[0, part], sibling)

    def sib_step(way, d, k):
        slot = sib_slot(way, d)
        part, side = ends(way, k)
        ref = tok.at[(z - slot) % 8, part, side]
        c = part * 2 + side
        return remote(ref, ref, sib_send.at[slot, c], sib_recv.at[slot, c], sibling)

    def sib_slot(way, d):
        return d if way == 0 else 8 - d

    def half_of(k):
        return zl if k == 0 else 1 - zl

    def w_step(way, d, k):
        shard = (y - (d - 1)) % 8 if way == 0 else (y + (d - 1)) % 8
        target = device((y + 1) % 8 if way == 0 else (y + 7) % 8, zh, x, zl, core)
        ref = wbuf.at[shard, half_of(k)]
        return remote(
            ref, ref, wr_send.at[way, d - 1, k], wr_recv.at[way, d - 1, k], target
        )

    def ws_step(slot, k):
        ref = wbuf.at[(y - slot) % 8, half_of(k), 0]
        return remote(ref, ref, ws_send.at[slot, k], ws_recv.at[slot, k], sibling)

    def wa_step(k, owner):
        source = wown.at[:, half_of(k) * 2 + owner]
        landing = wbuf.at[y, zl, owner, core]
        slot = k * 2 + core
        return remote(
            source, landing, wa_send.at[k, owner], wa_recv.at[slot, owner],
            device(y, zh, x, half_of(k), 1),
        )

    def wa_arrival(k, side, owner):
        landing = wbuf.at[y, half_of(k), owner, side]
        return remote(
            landing, landing, wa_send.at[k, owner], wa_recv.at[k * 2 + side, owner], sibling
        )

    for copy in own_tok:
        copy.wait()
    for part in range(2):
        swap_step(part).start()

    @pl.when(core == 0)
    def _():
        for way in range(2):
            tok_step(way, 1, 0).start()

    own_w.wait()
    for owner in range(2):
        wa_step(1, owner).start()

    @pl.when(core == 0)
    def _():
        for owner in range(2):
            wa_step(0, owner).start()

    @pl.when(core == 1)
    def _():
        for owner in range(2):
            wbuf[y, zl, owner, 1] = wown[:, zl * 2 + owner]

    @pl.when(core == 0)
    def _():
        for part in range(2):
            swap_step(part).wait_recv()
        for k in range(1, 4):
            for way in range(2):
                tok_step(way, 1, k).start()

    @pl.when(core == 1)
    def _():
        for owner in range(2):
            wa_arrival(0, 0, owner).wait_recv()
        for way in range(2):
            w_step(way, 1, 0).start()
        ws_step(0, 0).start()

    own_filt.wait()
    fstage[...] = filt[...].astype(BF16)
    for copy in own_params:
        copy.wait()
    pstage[...] = jnp.zeros_like(pstage)
    for i in range(3):
        for b in range(3):
            pstage[i * 3 + b : i * 3 + b + 1, :] = short[i, b : b + 1, :]
    pstage[9:10, :] = skip[...]

    def f_step(i):
        return remote(
            fstage.at[pl.ds(i * 16, 16)], fmid.at[zl, zh], f_send.at[i], f_recv.at[0],
            filter_holder(i),
        )

    def g_step(delta):
        target = (y + delta) % 8
        return remote(
            fturn.at[target], fbuf.at[y], g_send.at[delta], g_recv.at[0],
            device(target, zh, x, zl, core),
        )

    def p_step(delta):
        mate = (quarter + delta) % 4
        return remote(
            pstage, pbuf, p_send.at[delta], p_recv.at[0], device(y, zh, x, mate // 2, mate % 2)
        )

    @pl.when(mirrored)
    def _():
        pltpu.make_async_copy(pstage, pbuf, p_recv.at[0]).start()
        for delta in range(1, 4):
            p_step(delta).start()

    def pass_tokens(d, k):
        for way in range(2):
            tok_step(way, d, k).wait_recv()
            if d < 4 and goes(d + 1, way, k):
                tok_step(way, d + 1, k).start()
            sib_step(way, d, k).start()

    def pass_weights(d, k):
        for way in range(2):
            if w_goes(d, way, k):
                w_step(way, d, k).wait_recv()
                if d < 4 and w_goes(d + 1, way, k):
                    w_step(way, d + 1, k).start()
                ws_step(sib_slot(way, d), k).start()

    def await_tokens(d):
        @pl.when(core == 1)
        def _():
            if d == 0:
                for part in range(2):
                    swap_step(part).wait_recv()
            else:
                for k in range(4):
                    for way in range(2):
                        if goes(d, way, k):
                            sib_step(way, d, k).wait_recv()

    def await_weights(d):
        @pl.when(core == 0)
        def _():
            for k in range(2):
                for way in range(2):
                    if w_goes(d, way, k) and (d > 0 or way == 0):
                        ws_step(sib_slot(way, d) % 8, k).wait_recv()

    @pl.when(core == 0)
    def _():
        for d in range(1, 3):
            for k in range(4):
                pass_tokens(d, k)

    @pl.when(core == 1)
    def _():
        for side in range(2):
            for owner in range(2):
                wa_arrival(1, side, owner).wait_recv()
        for way in range(2):
            w_step(way, 1, 1).start()
        ws_step(0, 1).start()
        for d in range(1, 4):
            for k in range(2):
                pass_weights(d, k)

    sign = 2 * zl - 1
    blocks = [zh, (zh + sign) % 4, (zh - sign) % 4, (zh + 2) % 4]
    near = [[0], [1, 7], [2, 6], [3, 5], [4]]

    def x_step(p, row):
        return remote(
            sbuf.at[p, row], rbuf.at[p, x, row % 2], x_send.at[p, row], x_recv.at[p],
            device(y, zh, row // 2, zl, core),
        )

    def project(p, steps):
        rows = [(y + delta) % 8 for step in steps for delta in near[step]]
        total = jnp.zeros((48 * len(rows), 256), F32)
        for half in range(2):
            for side in range(2):
                left = jnp.concatenate(
                    [wbuf[row, half, core, side].reshape(48, 512) for row in rows], 0
                )
                right = tok[blocks[p] * 2 + half, :, side].reshape(256, 512)
                total = total + lax.dot_general(
                    left, right, (((1,), (1,)), ((), ())), preferred_element_type=F32
                )
        rounded = total.astype(BF16)
        for n, row in enumerate(rows):
            sbuf[p, row] = rounded[n * 48 : (n + 1) * 48, :]
        for row in rows:
            @pl.when(row // 2 != x)
            def _():
                x_step(p, row).start()

            @pl.when(row // 2 == x)
            def _():
                pltpu.make_async_copy(
                    sbuf.at[p, row], rbuf.at[p, x, row % 2], x_recv.at[p]
                ).start()

    def sum_over_x(p):
        pltpu.make_async_copy(rbuf.at[p], rbuf.at[p], x_recv.at[p]).wait()
        total = rbuf[p, 0].astype(F32)
        for n in range(1, 4):
            total = total + rbuf[p, n].astype(F32)
        total = total.reshape(96, 256)
        for j in range(2):
            sums[p, pl.ds(j, 96, stride=2), :] = total[:, j * 128 : (j + 1) * 128]

    def pieces(p, target):
        first_row = (target // 4) * 96 + (target % 4) * 8
        return [sums[p, first_row + b * 32 : first_row + b * 32 + 8, :] for b in range(3)]

    def e_step(delta):
        target = (y + delta) % 8
        return remote(
            aearly.at[target], xearly.at[y], e_send.at[delta], e_recv.at[0],
            device(target, zh, x, zl, core),
        )

    def a_step(delta):
        target = (y + delta) % 8
        return remote(
            alate.at[target], xlate.at[y], a_send.at[delta], a_recv.at[0],
            device(target, zh, x, zl, core),
        )

    def reduce_pair(first_block, packed, step, landed, arrived):
        for p in (first_block, first_block + 1):
            sum_over_x(p)
        for target in range(8):
            parts = pieces(first_block, target) + pieces(first_block + 1, target)
            packed[target] = jnp.concatenate(parts, 0).astype(BF16)
        for delta in FAR_FIRST:
            step(delta).start()
        pltpu.make_async_copy(packed.at[y], landed.at[y], arrived.at[0]).start()

    def reduce_early():
        reduce_pair(0, aearly, e_step, xearly, e_recv)

    def reduce_late():
        reduce_pair(2, alate, a_step, xlate, a_recv)

    def transform(value):
        stage = table_left(first[...], value)
        rows = []
        for ch in range(4):
            re = stage[:64, ch * 128 : (ch + 1) * 128]
            im = stage[64:, ch * 128 : (ch + 1) * 128]
            rows.append(
                jnp.concatenate(
                    [re * twist[0] + im * twist[1], im * twist[0] - re * twist[1]], 1
                )
            )
        return table_right(jnp.concatenate(rows, 0), second[...])

    @pl.when(core == 0)
    def _():
        for k in range(4):
            pass_tokens(3, k)

    await_tokens(0)
    await_tokens(1)
    for d in range(4):
        await_weights(d)
    project(0, [0, 1, 2, 3])
    await_tokens(2)
    project(1, [0, 1, 2, 3])

    @pl.when(core == 1)
    def _():
        for k in range(2):
            pass_weights(4, k)

    await_weights(4)
    project(0, [4])
    project(1, [4])
    await_tokens(3)
    project(2, [0, 1, 2, 3, 4])

    @pl.when(core == 0)
    def _():
        for k in range(2):
            pass_tokens(4, k)

    await_tokens(4)
    for i in range(8):
        @pl.when(jnp.logical_not(at_home & (own_block == i)))
        def _():
            f_step(i).start()

    @pl.when(at_home)
    def _():
        pltpu.make_async_copy(
            fstage.at[pl.ds(pl.multiple_of(own_block * 16, 16), 16)], fmid.at[zl, zh],
            f_recv.at[0],
        ).start()

    project(3, [0, 1, 2, 3, 4])
    reduce_early()

    pltpu.make_async_copy(fmid, fmid, f_recv.at[0]).wait()
    for side in range(2):
        for from_zh in range(4):
            piece = fmid[side, from_zh].astype(F32)
            for j in range(2):
                fwide[pl.ds(side * 128 + from_zh * 2 + j, 16, stride=8), :] = piece[
                    :, j * 128 : (j + 1) * 128
                ]
    fturn[...] = fwide[...].astype(BF16).reshape(8, 32, 128)
    for delta in FAR_FIRST:
        g_step(delta).start()
    pltpu.make_async_copy(fturn.at[y], fbuf.at[y], g_recv.at[0]).start()

    reduce_late()

    @pl.when(core == 0)
    def _():
        for owner in range(2):
            wa_step(0, owner).wait_send()
        for d in range(1, 5):
            for k in range(4):
                for way in range(2):
                    if goes(d, way, k):
                        tok_step(way, d, k).wait_send()
                        sib_step(way, d, k).wait_send()

    @pl.when(core == 1)
    def _():
        for k in range(2):
            ws_step(0, k).wait_send()
        for d in range(1, 5):
            for k in range(2):
                for way in range(2):
                    if w_goes(d, way, k):
                        w_step(way, d, k).wait_send()
                        ws_step(sib_slot(way, d), k).wait_send()

    for owner in range(2):
        wa_step(1, owner).wait_send()
        swap_step(owner).wait_send()
    for p in range(4):
        for row in range(8):
            @pl.when(row // 2 != x)
            def _():
                x_step(p, row).wait_send()

    pltpu.make_async_copy(fbuf, fbuf, g_recv.at[0]).wait()
    pltpu.make_async_copy(pbuf, pbuf, p_recv.at[0]).wait()
    for copy in own_tables:
        copy.wait()
    fwide[...] = fbuf[...].astype(F32).reshape(256, 128)
    lanes = []
    for ch in range(4):
        lanes.append(
            jnp.concatenate(
                [fwide[pl.ds(ch * 8 + inner, 8, stride=32), :] for inner in range(8)], 0
            )
        )
    spectrum[...] = transform(jnp.concatenate(lanes, 1)) * (1.0 / 8192.0)

    for delta in FAR_FIRST:
        e_step(delta).wait_send()
        g_step(delta).wait_send()

    @pl.when(mirrored)
    def _():
        for delta in range(1, 4):
            p_step(delta).wait_send()

    for i in range(8):
        @pl.when(jnp.logical_not(at_home & (own_block == i)))
        def _():
            f_step(i).wait_send()

    channel = 64 * (zh % 2) + 32 * zl + 16 * core + 4 * (y % 4)
    lane_at = lax.broadcasted_iota(jnp.int32, (16, 128), 1)
    gains = [
        jnp.sum(jnp.where(lane_at == channel + ch, pbuf[...], 0.0), axis=1, keepdims=True)
        for ch in range(4)
    ]
    pltpu.make_async_copy(xearly, xearly, e_recv.at[0]).wait()
    wide = xearly[...].astype(F32)
    for p in range(2):
        xwide[blocks[p]] = wide[:, p * 24 : (p + 1) * 24, :].reshape(192, 128)
    pltpu.make_async_copy(xlate, xlate, a_recv.at[0]).wait()
    wide = xlate[...].astype(F32)
    for p in range(2):
        xwide[blocks[2 + p]] = wide[:, p * 24 : (p + 1) * 24, :].reshape(192, 128)
    lane = lax.broadcasted_iota(jnp.int32, (64, 128), 1)
    below = lax.broadcasted_iota(jnp.int32, (8, 128), 0)

    def mixed(b, ch):
        here = jnp.concatenate(
            [
                xwide[inner // 2, pl.ds((b * 4 + ch) * 2 + inner % 2, 8, stride=24), :]
                for inner in range(8)
            ],
            0,
        )
        total = gains[ch][b : b + 1, :] * here
        for i in range(1, 3):
            turned = pltpu.roll(here, i, 1)
            wrapped = jnp.where(below == 0, 0.0, pltpu.roll(turned[56:, :], 1, 0))
            before = jnp.concatenate([wrapped, turned[:56, :]], 0)
            total = total + gains[ch][i * 3 + b : i * 3 + b + 1, :] * jnp.where(
                lane < i, before, turned
            )
        return total

    drives = [mixed(1, ch) * mixed(2, ch) for ch in range(4)]
    wave = transform(jnp.concatenate(drives, 1))
    wave_re, wave_im = wave[:, :128], wave[:, 128:]
    filt_re, filt_im = spectrum[:, :128], spectrum[:, 128:]
    product = jnp.concatenate(
        [wave_re * filt_re - wave_im * filt_im, wave_re * filt_im + wave_im * filt_re], 1
    )
    back = table_right(product, jnp.transpose(second[...], (1, 0)))
    columns = []
    for ch in range(4):
        re = back[ch * 64 : (ch + 1) * 64, :128]
        im = back[ch * 64 : (ch + 1) * 64, 128:]
        columns.append(
            jnp.concatenate(
                [re * twist[0] - im * twist[1], im * twist[0] + re * twist[1]], 0
            )
        )
    convolved = table_left(last[...], jnp.concatenate(columns, 1))
    for ch in range(4):
        gated = mixed(0, ch) * (
            convolved[:, ch * 128 : (ch + 1) * 128] + gains[ch][9:10, :] * drives[ch]
        )
        for inner in range(8):
            fwide[pl.ds(ch * 8 + inner, 8, stride=32), :] = gated[
                inner * 8 : (inner + 1) * 8, :
            ]

    oturn[...] = fwide[...].astype(BF16).reshape(8, 32, 128)

    def n_step(delta):
        target = (y + delta) % 8
        return remote(
            oturn.at[target], omid.at[y], n_send.at[delta], n_recv.at[0],
            device(target, zh, x, zl, core),
        )

    for delta in FAR_FIRST:
        n_step(delta).start()
    pltpu.make_async_copy(oturn.at[y], omid.at[y], n_recv.at[0]).start()

    out_rows = out.at[pl.ds(pl.multiple_of(own_block * 16, 16), 16)]

    def o_step(i):
        return remote(ostage.at[i], out_rows, o_send.at[i], o_recv.at[0], out_owner(i))

    pltpu.make_async_copy(omid, omid, n_recv.at[0]).wait()
    fwide[...] = omid[...].astype(F32).reshape(256, 128)
    for i in range(8):
        first_row = (i // 4) * 128 + (i % 4) * 2
        ostage[i] = jnp.concatenate(
            [fwide[pl.ds(first_row + j, 16, stride=8), :] for j in range(2)], 1
        ).astype(BF16)
    for i in range(8):
        @pl.when(jnp.logical_not(at_home & (own_out == i)))
        def _():
            o_step(i).start()

    @pl.when(at_home)
    def _():
        pltpu.make_async_copy(ostage.at[own_out], out_rows, o_recv.at[0]).start()

    for i in range(8):
        @pl.when(jnp.logical_not(at_home & (own_out == i)))
        def _():
            o_step(i).wait_send()

    for delta in FAR_FIRST:
        a_step(delta).wait_send()
        n_step(delta).wait_send()
    pltpu.make_async_copy(out, out, o_recv.at[0]).wait()


def per_device(tokens, in_weight, short_filter, long_filter, skip_gain):
    consts = [jnp.asarray(table) for table in tables()]
    dma = pltpu.SemaphoreType.DMA
    hbm = pl.BlockSpec(memory_space=pltpu.HBM)
    columns = jnp.transpose(in_weight, (0, 2, 1)).reshape(3, 4, 16, 512)
    return pl.pallas_call(
        kernel,
        out_shape=jax.ShapeDtypeStruct((128, 256), BF16),
        in_specs=[hbm] * 9,
        out_specs=hbm,
        scratch_shapes=[
            pltpu.VMEM((128, 64), F32),
            pltpu.VMEM((2, 64, 128), F32),
            pltpu.VMEM((256, 256), F32),
            pltpu.VMEM((64, 128), F32),
            pltpu.VMEM((3, 3, 128), F32),
            pltpu.VMEM((1, 128), F32),
            pltpu.VMEM((128, 256), F32),
            pltpu.VMEM((8, 2, 2, 128, 512), BF16),
            pltpu.VMEM((3, 4, 16, 512), BF16),
            pltpu.VMEM((8, 2, 2, 2, 3, 16, 512), BF16),
            pltpu.VMEM((4, 8, 48, 256), BF16),
            pltpu.VMEM((4, 4, 2, 48, 256), BF16),
            pltpu.VMEM((4, 192, 128), F32),
            pltpu.VMEM((8, 48, 128), BF16),
            pltpu.VMEM((8, 48, 128), BF16),
            pltpu.VMEM((8, 48, 128), BF16),
            pltpu.VMEM((8, 48, 128), BF16),
            pltpu.VMEM((4, 192, 128), F32),
            pltpu.VMEM((128, 256), BF16),
            pltpu.VMEM((2, 4, 16, 256), BF16),
            pltpu.VMEM((256, 128), F32),
            pltpu.VMEM((8, 32, 128), BF16),
            pltpu.VMEM((8, 32, 128), BF16),
            pltpu.VMEM((16, 128), F32),
            pltpu.VMEM((16, 128), F32),
            pltpu.VMEM((256, 256), F32),
            pltpu.VMEM((8, 32, 128), BF16),
            pltpu.VMEM((8, 32, 128), BF16),
            pltpu.VMEM((8, 16, 256), BF16),
            dma((1,)), dma((2,)), dma((1,)), dma((2,)), dma((4,)),
            dma((2, 4, 4)), dma((2, 4, 4)),
            dma((8, 4)), dma((8, 4)),
            dma((2, 2)), dma((4, 2)),
            dma((2, 4, 2)), dma((2, 4, 2)),
            dma((8, 2)), dma((8, 2)),
            dma((4, 8)), dma((4,)),
            dma((8,)), dma((1,)),
            dma((8,)), dma((1,)),
            dma((8,)), dma((1,)),
            dma((8,)), dma((1,)),
            dma((4,)), dma((1,)),
            dma((8,)), dma((1,)),
            dma((8,)), dma((1,)),
        ],
        compiler_params=pltpu.CompilerParams(
            collective_id=0, has_side_effects=True, vmem_limit_bytes=63 * 1024 * 1024
        ),
    )(tokens.reshape(2, 128, 512), columns, short_filter, long_filter, skip_gain[None, :], *consts)


def solution(mesh):
    placed = (
        P("seq", "chan"),
        P(None, "chan", "seq"),
        P(None, None, "chan"),
        P("chan", "seq"),
        P("chan"),
    )
    return jax.shard_map(
        per_device, mesh=mesh, in_specs=placed, out_specs=P("chan", "seq"), check_vma=False
    )
```

```python
import jax
import jax.numpy as jnp
import numpy as np
from jax import lax
from jax.experimental import pallas as pl
from jax.experimental.pallas import tpu as pltpu
from jax.sharding import PartitionSpec as P

MESH = pl.DeviceIdType.MESH
F32 = jnp.float32
FAR_FIRST = (4, 3, 5, 2, 6, 1, 7)
BF16 = jnp.bfloat16


def tables():
    row = np.arange(64)
    outer = 8 * (row % 8) + row // 8
    freq = np.arange(64) + 0.25
    lane = np.arange(128)
    chi = 2 * np.pi * np.outer(freq, outer) / 64
    phi = 2 * np.pi * np.outer(freq, lane) / 8192
    psi = 2 * np.pi * np.outer(lane, lane) / 128
    first = np.concatenate([np.cos(chi), -np.sin(chi)], 0)
    twist = np.stack([np.cos(phi), np.sin(phi)]).astype(np.float32)
    second = np.block([[np.cos(psi), -np.sin(psi)], [np.sin(psi), np.cos(psi)]])
    last = np.concatenate([np.cos(chi).T, -np.sin(chi).T], 1)
    return (
        first.astype(np.float32),
        twist,
        second.astype(np.float32),
        last.astype(np.float32),
    )


def split(value):
    high = value.astype(BF16)
    return high, (value - high.astype(F32)).astype(BF16)


def dot(left, right):
    return jnp.dot(left, right, preferred_element_type=F32)


def table_left(table, value):
    table = split(table)
    high, low = split(value)
    return dot(table[0], high) + (dot(table[0], low) + dot(table[1], high))


def table_right(value, table):
    table = split(table)
    high, low = split(value)
    return dot(high, table[0]) + (dot(low, table[0]) + dot(high, table[1]))


def kernel(
    tok_in, w_in, short_in, filt_in, skip_in, first_in, twist_in, second_in, last_in,
    out,
    first, twist, second, last, short, skip, filt,
    tok, wown, wbuf, sbuf, rbuf, sums, aearly, xearly, alate, xlate, xwide,
    fstage, fmid, fwide, fturn, fbuf, pstage, pbuf, spectrum, owide, oturn, omid, ostage,
    in_sem, tok_sem, own_sem, param_sem, table_sem,
    tok_send, tok_recv, sib_send, sib_recv, wa_send, wa_recv, wr_send, wr_recv,
    ws_send, ws_recv,
    x_send, x_recv, e_send, e_recv, a_send, a_recv, f_send, f_recv, g_send, g_recv, p_send, p_recv,
    n_send, n_recv, o_send, o_recv,
):
    seq, chan = lax.axis_index("seq"), lax.axis_index("chan")
    y, zh = seq // 4, seq % 4
    x, zl, core = chan // 4, (chan // 2) % 2, chan % 2
    z = zh * 2 + zl

    def device(y_, zh_, x_, zl_, core_):
        return (y_ * 4 + zh_, (x_ * 2 + zl_) * 2 + core_)

    def device_z(z_):
        return device(y, z_ // 2, x, z_ % 2, core)

    sibling = device(y, zh, x, zl, 1 - core)
    mirrored = (zl == y // 4) & (core == zh // 2)

    def filter_holder(i):
        return device(y, 2 * core + i // 4, x, (i // 2) % 2, i % 2)

    def out_owner(i):
        return device(y, i % 4, x, i // 4, zh // 2)

    at_home = core == zh // 2
    own_block = (zh % 2) * 4 + zl * 2 + core
    between = zl == y // 4
    own_out = zl * 4 + zh

    barrier = pltpu.get_barrier_semaphore()

    def greet(target):
        pl.semaphore_signal(barrier, inc=1, device_id=target, device_id_type=MESH)

    @pl.when(core == 0)
    def _():
        greet(device_z((z + 1) % 8))
        greet(device_z((z + 7) % 8))

    @pl.when(core == 1)
    def _():
        greet(device((y + 1) % 8, zh, x, zl, core))
        greet(device((y + 7) % 8, zh, x, zl, core))

    for delta in range(1, 4):
        mate = (zl * 2 + core + delta) % 4
        greet(device(y, zh, x, mate // 2, mate % 2))
        greet(device(y, zh, (x + delta) % 4, zl, core))

    quarter = zl * 2 + core
    own_tok = [
        pltpu.make_async_copy(tok_in.at[c], tok.at[z, c, core], tok_sem.at[c]) for c in range(2)
    ]
    own_w = pltpu.make_async_copy(w_in, wown, own_sem.at[0])
    own_filt = [
        pltpu.make_async_copy(filt_in.at[:, pl.ds(j * 128, 128)], filt.at[j], in_sem.at[j])
        for j in range(2)
    ]
    own_params = [
        pltpu.make_async_copy(short_in, short, param_sem.at[0]),
        pltpu.make_async_copy(skip_in, skip, param_sem.at[1]),
    ]
    own_tables = [
        pltpu.make_async_copy(first_in, first, table_sem.at[0]),
        pltpu.make_async_copy(twist_in, twist, table_sem.at[1]),
        pltpu.make_async_copy(second_in, second, table_sem.at[2]),
        pltpu.make_async_copy(last_in, last, table_sem.at[3]),
    ]
    for copy in own_tok + [own_w] + own_filt + own_params + own_tables:
        copy.start()

    pl.semaphore_wait(barrier, 8)

    def remote(src, dst, send, recv, target):
        return pltpu.make_async_remote_copy(
            src_ref=src, dst_ref=dst, send_sem=send, recv_sem=recv,
            device_id=target, device_id_type=MESH,
        )

    def ends(way, k):
        return k // 2 ^ way, k % 2

    def goes(d, way, k):
        return d < 4 or k < 2

    def w_goes(d, way, k):
        return d < 4 or k == way

    def tok_step(way, d, k):
        shard = (z - (d - 1)) % 8 if way == 0 else (z + (d - 1)) % 8
        target = device_z((z + 1) % 8 if way == 0 else (z + 7) % 8)
        part, side = ends(way, k)
        ref = tok.at[shard, part, side]
        return remote(
            ref, ref, tok_send.at[way, d - 1, k], tok_recv.at[way, d - 1, k], target
        )

    def swap_step(part):
        ref = tok.at[z, part, core]
        return remote(ref, ref, sib_send.at[0, part], sib_recv.at[0, part], sibling)

    def sib_step(way, d, k):
        slot = sib_slot(way, d)
        part, side = ends(way, k)
        ref = tok.at[(z - slot) % 8, part, side]
        c = part * 2 + side
        return remote(ref, ref, sib_send.at[slot, c], sib_recv.at[slot, c], sibling)

    def sib_slot(way, d):
        return d if way == 0 else 8 - d

    def half_of(k):
        return zl if k == 0 else 1 - zl

    def w_step(way, d, k):
        shard = (y - (d - 1)) % 8 if way == 0 else (y + (d - 1)) % 8
        target = device((y + 1) % 8 if way == 0 else (y + 7) % 8, zh, x, zl, core)
        ref = wbuf.at[shard, half_of(k)]
        return remote(
            ref, ref, wr_send.at[way, d - 1, k], wr_recv.at[way, d - 1, k], target
        )

    def ws_step(slot, k):
        ref = wbuf.at[(y - slot) % 8, half_of(k), 0]
        return remote(ref, ref, ws_send.at[slot, k], ws_recv.at[slot, k], sibling)

    def wa_step(k, owner):
        source = wown.at[:, half_of(k) * 2 + owner]
        landing = wbuf.at[y, zl, owner, core]
        slot = k * 2 + core
        return remote(
            source, landing, wa_send.at[k, owner], wa_recv.at[slot, owner],
            device(y, zh, x, half_of(k), 1),
        )

    def wa_arrival(k, side, owner):
        landing = wbuf.at[y, half_of(k), owner, side]
        return remote(
            landing, landing, wa_send.at[k, owner], wa_recv.at[k * 2 + side, owner], sibling
        )

    for copy in own_tok:
        copy.wait()
    for part in range(2):
        swap_step(part).start()

    @pl.when(core == 0)
    def _():
        for way in range(2):
            tok_step(way, 1, 0).start()

    own_w.wait()
    for owner in range(2):
        wa_step(1, owner).start()

    @pl.when(core == 0)
    def _():
        for owner in range(2):
            wa_step(0, owner).start()

    @pl.when(core == 1)
    def _():
        for owner in range(2):
            wbuf[y, zl, owner, 1] = wown[:, zl * 2 + owner]

    @pl.when(core == 0)
    def _():
        for part in range(2):
            swap_step(part).wait_recv()
        for k in range(1, 4):
            for way in range(2):
                tok_step(way, 1, k).start()

    @pl.when(core == 1)
    def _():
        for owner in range(2):
            wa_arrival(0, 0, owner).wait_recv()
        for way in range(2):
            w_step(way, 1, 0).start()
        ws_step(0, 0).start()

    for copy in own_filt:
        copy.wait()
    for k in range(4):
        tiles = [
            filt[j, pl.ds(k * 4 + ch, 8, stride=16), :]
            for ch in range(4)
            for j in range(2)
        ]
        fstage[k] = jnp.concatenate(tiles, 0).astype(BF16)
    for copy in own_params:
        copy.wait()
    pstage[...] = jnp.zeros_like(pstage)
    for i in range(3):
        for b in range(3):
            pstage[i * 3 + b : i * 3 + b + 1, :] = short[i, b : b + 1, :]
    pstage[9:10, :] = skip[...]

    def f_step(k):
        return remote(
            fstage.at[k], fmid.at[y], f_send.at[k], f_recv.at[0],
            device(4 * zl + k, zh, x, zl, core),
        )

    def g_step(i):
        return remote(
            fturn.at[i], fbuf.at[zh], g_send.at[i], g_recv.at[0], filter_holder(i)
        )

    def p_step(delta):
        mate = (quarter + delta) % 4
        return remote(
            pstage, pbuf, p_send.at[delta], p_recv.at[0], device(y, zh, x, mate // 2, mate % 2)
        )

    @pl.when(mirrored)
    def _():
        pltpu.make_async_copy(pstage, pbuf, p_recv.at[0]).start()
        for delta in range(1, 4):
            p_step(delta).start()

    def pass_tokens(d, k):
        for way in range(2):
            tok_step(way, d, k).wait_recv()
            if d < 4 and goes(d + 1, way, k):
                tok_step(way, d + 1, k).start()
            sib_step(way, d, k).start()

    def pass_weights(d, k):
        for way in range(2):
            if w_goes(d, way, k):
                w_step(way, d, k).wait_recv()
                if d < 4 and w_goes(d + 1, way, k):
                    w_step(way, d + 1, k).start()
                ws_step(sib_slot(way, d), k).start()

    def await_tokens(d):
        @pl.when(core == 1)
        def _():
            if d == 0:
                for part in range(2):
                    swap_step(part).wait_recv()
            else:
                for k in range(4):
                    for way in range(2):
                        if goes(d, way, k):
                            sib_step(way, d, k).wait_recv()

    def await_weights(d):
        @pl.when(core == 0)
        def _():
            for k in range(2):
                for way in range(2):
                    if w_goes(d, way, k) and (d > 0 or way == 0):
                        ws_step(sib_slot(way, d) % 8, k).wait_recv()

    @pl.when(core == 0)
    def _():
        for d in range(1, 3):
            for k in range(4):
                pass_tokens(d, k)

    @pl.when(core == 1)
    def _():
        for side in range(2):
            for owner in range(2):
                wa_arrival(1, side, owner).wait_recv()
        for way in range(2):
            w_step(way, 1, 1).start()
        ws_step(0, 1).start()
        for d in range(1, 4):
            for k in range(2):
                pass_weights(d, k)

    sign = 2 * zl - 1
    blocks = [zh, (zh + sign) % 4, (zh - sign) % 4, (zh + 2) % 4]
    near = [[0], [1, 7], [2, 6], [3, 5], [4]]

    def x_step(p, row):
        return remote(
            sbuf.at[p, row], rbuf.at[p, x, row % 2], x_send.at[p, row], x_recv.at[p],
            device(y, zh, row // 2, zl, core),
        )

    def project(p, steps):
        rows = [(y + delta) % 8 for step in steps for delta in near[step]]
        total = jnp.zeros((48 * len(rows), 256), F32)
        for half in range(2):
            for side in range(2):
                left = jnp.concatenate(
                    [wbuf[row, half, core, side].reshape(48, 512) for row in rows], 0
                )
                right = tok[blocks[p] * 2 + half, :, side].reshape(256, 512)
                total = total + lax.dot_general(
                    left, right, (((1,), (1,)), ((), ())), preferred_element_type=F32
                )
        rounded = total.astype(BF16)
        for n, row in enumerate(rows):
            sbuf[p, row] = rounded[n * 48 : (n + 1) * 48, :]
        for row in rows:
            @pl.when(row // 2 != x)
            def _():
                x_step(p, row).start()

            @pl.when(row // 2 == x)
            def _():
                pltpu.make_async_copy(
                    sbuf.at[p, row], rbuf.at[p, x, row % 2], x_recv.at[p]
                ).start()

    def sum_over_x(p):
        pltpu.make_async_copy(rbuf.at[p], rbuf.at[p], x_recv.at[p]).wait()
        total = rbuf[p, 0].astype(F32)
        for n in range(1, 4):
            total = total + rbuf[p, n].astype(F32)
        total = total.reshape(96, 256)
        for j in range(2):
            sums[p, pl.ds(j, 96, stride=2), :] = total[:, j * 128 : (j + 1) * 128]

    def pieces(p, target):
        first_row = (target // 4) * 96 + (target % 4) * 8
        return [sums[p, first_row + b * 32 : first_row + b * 32 + 8, :] for b in range(3)]

    def e_step(delta):
        target = (y + delta) % 8
        return remote(
            aearly.at[target], xearly.at[y], e_send.at[delta], e_recv.at[0],
            device(target, zh, x, zl, core),
        )

    def a_step(delta):
        target = (y + delta) % 8
        return remote(
            alate.at[target], xlate.at[y], a_send.at[delta], a_recv.at[0],
            device(target, zh, x, zl, core),
        )

    def reduce_pair(first_block, packed, step, landed, arrived):
        for p in (first_block, first_block + 1):
            sum_over_x(p)
        for target in range(8):
            parts = pieces(first_block, target) + pieces(first_block + 1, target)
            packed[target] = jnp.concatenate(parts, 0).astype(BF16)
        for delta in FAR_FIRST:
            step(delta).start()
        pltpu.make_async_copy(packed.at[y], landed.at[y], arrived.at[0]).start()

    def reduce_early():
        reduce_pair(0, aearly, e_step, xearly, e_recv)

    def reduce_late():
        reduce_pair(2, alate, a_step, xlate, a_recv)

    def transform(value):
        stage = table_left(first[...], value)
        rows = []
        for ch in range(4):
            re = stage[:64, ch * 128 : (ch + 1) * 128]
            im = stage[64:, ch * 128 : (ch + 1) * 128]
            rows.append(
                jnp.concatenate(
                    [re * twist[0] + im * twist[1], im * twist[0] - re * twist[1]], 1
                )
            )
        return table_right(jnp.concatenate(rows, 0), second[...])

    @pl.when(core == 0)
    def _():
        for k in range(4):
            pass_tokens(3, k)

    await_tokens(0)
    await_tokens(1)
    for d in range(4):
        await_weights(d)
    project(0, [0, 1, 2, 3])
    await_tokens(2)
    project(1, [0, 1, 2, 3])

    @pl.when(core == 1)
    def _():
        for k in range(2):
            pass_weights(4, k)

    await_weights(4)
    for k in range(4):
        @pl.when(4 * zl + k != y)
        def _():
            f_step(k).start()

    @pl.when(between)
    def _():
        pltpu.make_async_copy(fstage.at[y % 4], fmid.at[y], f_recv.at[0]).start()

    project(0, [4])
    project(1, [4])
    await_tokens(3)
    project(2, [0, 1, 2, 3, 4])

    @pl.when(core == 0)
    def _():
        for k in range(2):
            pass_tokens(4, k)

    await_tokens(4)
    project(3, [0, 1, 2, 3, 4])
    @pl.when(between)
    def _():
        pltpu.make_async_copy(fmid, fmid, f_recv.at[0]).wait()
        fwide[...] = fmid[...].astype(F32).reshape(512, 128)
        for i in range(8):
            tiles = [fwide[pl.ds(n * 8 + i, 8, stride=64), :] for n in range(8)]
            fturn[i] = jnp.concatenate(tiles, 0).astype(BF16)
        for i in range(8):
            @pl.when(jnp.logical_not(at_home & (own_block == i)))
            def _():
                g_step(i).start()

        @pl.when(at_home)
        def _():
            pltpu.make_async_copy(fturn.at[own_block], fbuf.at[zh], g_recv.at[0]).start()

    reduce_early()

    reduce_late()

    @pl.when(core == 0)
    def _():
        for owner in range(2):
            wa_step(0, owner).wait_send()
        for d in range(1, 5):
            for k in range(4):
                for way in range(2):
                    if goes(d, way, k):
                        tok_step(way, d, k).wait_send()
                        sib_step(way, d, k).wait_send()

    @pl.when(core == 1)
    def _():
        for k in range(2):
            ws_step(0, k).wait_send()
        for d in range(1, 5):
            for k in range(2):
                for way in range(2):
                    if w_goes(d, way, k):
                        w_step(way, d, k).wait_send()
                        ws_step(sib_slot(way, d), k).wait_send()

    for owner in range(2):
        wa_step(1, owner).wait_send()
        swap_step(owner).wait_send()
    for p in range(4):
        for row in range(8):
            @pl.when(row // 2 != x)
            def _():
                x_step(p, row).wait_send()

    pltpu.make_async_copy(fbuf, fbuf, g_recv.at[0]).wait()
    pltpu.make_async_copy(pbuf, pbuf, p_recv.at[0]).wait()
    for copy in own_tables:
        copy.wait()
    wide = fbuf[...].astype(F32)
    lanes = []
    for ch in range(4):
        lanes.append(
            jnp.concatenate(
                [wide[n, (ch * 2 + j) * 8 : (ch * 2 + j + 1) * 8, :] for n in range(4) for j in range(2)],
                0,
            )
        )
    spectrum[...] = transform(jnp.concatenate(lanes, 1)) * (1.0 / 8192.0)

    for delta in FAR_FIRST:
        e_step(delta).wait_send()

    @pl.when(mirrored)
    def _():
        for delta in range(1, 4):
            p_step(delta).wait_send()

    for k in range(4):
        @pl.when(4 * zl + k != y)
        def _():
            f_step(k).wait_send()

    for i in range(8):
        @pl.when(between & jnp.logical_not(at_home & (own_block == i)))
        def _():
            g_step(i).wait_send()

    channel = 64 * (zh % 2) + 32 * zl + 16 * core + 4 * (y % 4)
    lane_at = lax.broadcasted_iota(jnp.int32, (16, 128), 1)
    gains = [
        jnp.sum(jnp.where(lane_at == channel + ch, pbuf[...], 0.0), axis=1, keepdims=True)
        for ch in range(4)
    ]
    pltpu.make_async_copy(xearly, xearly, e_recv.at[0]).wait()
    wide = xearly[...].astype(F32)
    for p in range(2):
        xwide[blocks[p]] = wide[:, p * 24 : (p + 1) * 24, :].reshape(192, 128)
    pltpu.make_async_copy(xlate, xlate, a_recv.at[0]).wait()
    wide = xlate[...].astype(F32)
    for p in range(2):
        xwide[blocks[2 + p]] = wide[:, p * 24 : (p + 1) * 24, :].reshape(192, 128)
    lane = lax.broadcasted_iota(jnp.int32, (64, 128), 1)
    below = lax.broadcasted_iota(jnp.int32, (8, 128), 0)

    def mixed(b, ch):
        here = jnp.concatenate(
            [
                xwide[inner // 2, pl.ds((b * 4 + ch) * 2 + inner % 2, 8, stride=24), :]
                for inner in range(8)
            ],
            0,
        )
        total = gains[ch][b : b + 1, :] * here
        for i in range(1, 3):
            turned = pltpu.roll(here, i, 1)
            wrapped = jnp.where(below == 0, 0.0, pltpu.roll(turned[56:, :], 1, 0))
            before = jnp.concatenate([wrapped, turned[:56, :]], 0)
            total = total + gains[ch][i * 3 + b : i * 3 + b + 1, :] * jnp.where(
                lane < i, before, turned
            )
        return total

    drives = [mixed(1, ch) * mixed(2, ch) for ch in range(4)]
    wave = transform(jnp.concatenate(drives, 1))
    wave_re, wave_im = wave[:, :128], wave[:, 128:]
    filt_re, filt_im = spectrum[:, :128], spectrum[:, 128:]
    product = jnp.concatenate(
        [wave_re * filt_re - wave_im * filt_im, wave_re * filt_im + wave_im * filt_re], 1
    )
    back = table_right(product, jnp.transpose(second[...], (1, 0)))
    columns = []
    for ch in range(4):
        re = back[ch * 64 : (ch + 1) * 64, :128]
        im = back[ch * 64 : (ch + 1) * 64, 128:]
        columns.append(
            jnp.concatenate(
                [re * twist[0] - im * twist[1], im * twist[0] + re * twist[1]], 0
            )
        )
    convolved = table_left(last[...], jnp.concatenate(columns, 1))
    for ch in range(4):
        gated = mixed(0, ch) * (
            convolved[:, ch * 128 : (ch + 1) * 128] + gains[ch][9:10, :] * drives[ch]
        )
        for inner in range(8):
            owide[pl.ds(ch * 8 + inner, 8, stride=32), :] = gated[
                inner * 8 : (inner + 1) * 8, :
            ]

    oturn[...] = owide[...].astype(BF16).reshape(8, 32, 128)

    def n_step(delta):
        target = (y + delta) % 8
        return remote(
            oturn.at[target], omid.at[y], n_send.at[delta], n_recv.at[0],
            device(target, zh, x, zl, core),
        )

    for delta in FAR_FIRST:
        n_step(delta).start()
    pltpu.make_async_copy(oturn.at[y], omid.at[y], n_recv.at[0]).start()

    out_rows = out.at[pl.ds(pl.multiple_of(own_block * 16, 16), 16)]

    def o_step(i):
        return remote(ostage.at[i], out_rows, o_send.at[i], o_recv.at[0], out_owner(i))

    pltpu.make_async_copy(omid, omid, n_recv.at[0]).wait()
    owide[...] = omid[...].astype(F32).reshape(256, 128)
    for i in range(8):
        first_row = (i // 4) * 128 + (i % 4) * 2
        ostage[i] = jnp.concatenate(
            [owide[pl.ds(first_row + j, 16, stride=8), :] for j in range(2)], 1
        ).astype(BF16)
    for i in range(8):
        @pl.when(jnp.logical_not(at_home & (own_out == i)))
        def _():
            o_step(i).start()

    @pl.when(at_home)
    def _():
        pltpu.make_async_copy(ostage.at[own_out], out_rows, o_recv.at[0]).start()

    for i in range(8):
        @pl.when(jnp.logical_not(at_home & (own_out == i)))
        def _():
            o_step(i).wait_send()

    for delta in FAR_FIRST:
        a_step(delta).wait_send()
        n_step(delta).wait_send()
    pltpu.make_async_copy(out, out, o_recv.at[0]).wait()


def per_device(tokens, in_weight, short_filter, long_filter, skip_gain):
    consts = [jnp.asarray(table) for table in tables()]
    dma = pltpu.SemaphoreType.DMA
    hbm = pl.BlockSpec(memory_space=pltpu.HBM)
    columns = jnp.transpose(in_weight, (0, 2, 1)).reshape(3, 4, 16, 512)
    return pl.pallas_call(
        kernel,
        out_shape=jax.ShapeDtypeStruct((128, 256), BF16),
        in_specs=[hbm] * 9,
        out_specs=hbm,
        scratch_shapes=[
            pltpu.VMEM((128, 64), F32),
            pltpu.VMEM((2, 64, 128), F32),
            pltpu.VMEM((256, 256), F32),
            pltpu.VMEM((64, 128), F32),
            pltpu.VMEM((3, 3, 128), F32),
            pltpu.VMEM((1, 128), F32),
            pltpu.VMEM((2, 128, 128), F32),
            pltpu.VMEM((8, 2, 2, 128, 512), BF16),
            pltpu.VMEM((3, 4, 16, 512), BF16),
            pltpu.VMEM((8, 2, 2, 2, 3, 16, 512), BF16),
            pltpu.VMEM((4, 8, 48, 256), BF16),
            pltpu.VMEM((4, 4, 2, 48, 256), BF16),
            pltpu.VMEM((4, 192, 128), F32),
            pltpu.VMEM((8, 48, 128), BF16),
            pltpu.VMEM((8, 48, 128), BF16),
            pltpu.VMEM((8, 48, 128), BF16),
            pltpu.VMEM((8, 48, 128), BF16),
            pltpu.VMEM((4, 192, 128), F32),
            pltpu.VMEM((4, 64, 128), BF16),
            pltpu.VMEM((8, 64, 128), BF16),
            pltpu.VMEM((512, 128), F32),
            pltpu.VMEM((8, 64, 128), BF16),
            pltpu.VMEM((4, 64, 128), BF16),
            pltpu.VMEM((16, 128), F32),
            pltpu.VMEM((16, 128), F32),
            pltpu.VMEM((256, 256), F32),
            pltpu.VMEM((256, 128), F32),
            pltpu.VMEM((8, 32, 128), BF16),
            pltpu.VMEM((8, 32, 128), BF16),
            pltpu.VMEM((8, 16, 256), BF16),
            dma((2,)), dma((2,)), dma((1,)), dma((2,)), dma((4,)),
            dma((2, 4, 4)), dma((2, 4, 4)),
            dma((8, 4)), dma((8, 4)),
            dma((2, 2)), dma((4, 2)),
            dma((2, 4, 2)), dma((2, 4, 2)),
            dma((8, 2)), dma((8, 2)),
            dma((4, 8)), dma((4,)),
            dma((8,)), dma((1,)),
            dma((8,)), dma((1,)),
            dma((4,)), dma((1,)),
            dma((8,)), dma((1,)),
            dma((4,)), dma((1,)),
            dma((8,)), dma((1,)),
            dma((8,)), dma((1,)),
        ],
        compiler_params=pltpu.CompilerParams(
            collective_id=0, has_side_effects=True, vmem_limit_bytes=63 * 1024 * 1024
        ),
    )(tokens.reshape(2, 128, 512), columns, short_filter, long_filter, skip_gain[None, :], *consts)


def solution(mesh):
    placed = (
        P("seq", "chan"),
        P(None, "chan", "seq"),
        P(None, None, "chan"),
        P("chan", "seq"),
        P("chan"),
    )
    return jax.shard_map(
        per_device, mesh=mesh, in_specs=placed, out_specs=P("chan", "seq"), check_vma=False
    )
```

```python
import jax
import jax.numpy as jnp
import numpy as np
from jax import lax
from jax.experimental import pallas as pl
from jax.experimental.pallas import tpu as pltpu
from jax.sharding import PartitionSpec as P

MESH = pl.DeviceIdType.MESH
F32 = jnp.float32
FAR_FIRST = (4, 3, 5, 2, 6, 1, 7)
BF16 = jnp.bfloat16


def tables():
    row = np.arange(64)
    outer = 8 * (row % 8) + row // 8
    freq = np.arange(64) + 0.25
    lane = np.arange(128)
    chi = 2 * np.pi * np.outer(freq, outer) / 64
    phi = 2 * np.pi * np.outer(freq, lane) / 8192
    psi = 2 * np.pi * np.outer(lane, lane) / 128
    first = np.concatenate([np.cos(chi), -np.sin(chi)], 0)
    twist = np.stack([np.cos(phi), np.sin(phi)]).astype(np.float32)
    second = np.block([[np.cos(psi), -np.sin(psi)], [np.sin(psi), np.cos(psi)]])
    last = np.concatenate([np.cos(chi).T, -np.sin(chi).T], 1)
    return (
        first.astype(np.float32),
        twist,
        second.astype(np.float32),
        last.astype(np.float32),
    )


def split(value):
    high = value.astype(BF16)
    return high, (value - high.astype(F32)).astype(BF16)


def dot(left, right):
    return jnp.dot(left, right, preferred_element_type=F32)


def table_left(table, value):
    table = split(table)
    high, low = split(value)
    return dot(table[0], high) + (dot(table[0], low) + dot(table[1], high))


def table_right(value, table):
    table = split(table)
    high, low = split(value)
    return dot(high, table[0]) + (dot(low, table[0]) + dot(high, table[1]))


def kernel(
    tok_in, w_in, short_in, filt_in, skip_in, first_in, twist_in, second_in, last_in,
    out,
    first, twist, second, last, short, skip, filt,
    tok, wown, wbuf, sbuf, rbuf, sums, aearly, xearly, alate, xlate, xwide,
    fstage, fmid, fwide, fturn, fbuf, pstage, pbuf, spectrum, owide, oturn, omid, ostage,
    in_sem, tok_sem, own_sem, param_sem, table_sem,
    tok_send, tok_recv, sib_send, sib_recv, wa_send, wa_recv, wr_send, wr_recv,
    ws_send, ws_recv,
    x_send, x_recv, e_send, e_recv, a_send, a_recv, f_send, f_recv, g_send, g_recv, p_send, p_recv,
    n_send, n_recv, o_send, o_recv,
):
    seq, chan = lax.axis_index("seq"), lax.axis_index("chan")
    y, zh = seq // 4, seq % 4
    x, zl, core = chan // 4, (chan // 2) % 2, chan % 2
    z = zh * 2 + zl

    def device(y_, zh_, x_, zl_, core_):
        return (y_ * 4 + zh_, (x_ * 2 + zl_) * 2 + core_)

    def device_z(z_):
        return device(y, z_ // 2, x, z_ % 2, core)

    sibling = device(y, zh, x, zl, 1 - core)
    mirrored = (zl == y // 4) & (core == zh // 2)

    def filter_holder(i):
        return device(y, 2 * core + i // 4, x, (i // 2) % 2, i % 2)

    def out_owner(i):
        return device(y, i % 4, x, i // 4, zh // 2)

    at_home = core == zh // 2
    own_block = (zh % 2) * 4 + zl * 2 + core
    between = zl == y // 4
    own_out = zl * 4 + zh

    barrier = pltpu.get_barrier_semaphore()

    def greet(target):
        pl.semaphore_signal(barrier, inc=1, device_id=target, device_id_type=MESH)

    @pl.when(core == 0)
    def _():
        greet(device_z((z + 1) % 8))
        greet(device_z((z + 7) % 8))

    @pl.when(core == 1)
    def _():
        greet(device((y + 1) % 8, zh, x, zl, core))
        greet(device((y + 7) % 8, zh, x, zl, core))

    for delta in range(1, 4):
        mate = (zl * 2 + core + delta) % 4
        greet(device(y, zh, x, mate // 2, mate % 2))
        greet(device(y, zh, (x + delta) % 4, zl, core))

    quarter = zl * 2 + core
    own_tok = [
        pltpu.make_async_copy(tok_in.at[c], tok.at[z, c, core], tok_sem.at[c]) for c in range(2)
    ]
    own_w = pltpu.make_async_copy(w_in, wown, own_sem.at[0])
    own_filt = [
        pltpu.make_async_copy(filt_in.at[:, pl.ds(j * 128, 128)], filt.at[j], in_sem.at[j])
        for j in range(2)
    ]
    own_params = [
        pltpu.make_async_copy(short_in, short, param_sem.at[0]),
        pltpu.make_async_copy(skip_in, skip, param_sem.at[1]),
    ]
    own_tables = [
        pltpu.make_async_copy(first_in, first, table_sem.at[0]),
        pltpu.make_async_copy(twist_in, twist, table_sem.at[1]),
        pltpu.make_async_copy(second_in, second, table_sem.at[2]),
        pltpu.make_async_copy(last_in, last, table_sem.at[3]),
    ]
    for copy in own_tok + [own_w] + own_filt + own_params + own_tables:
        copy.start()

    pl.semaphore_wait(barrier, 8)

    def remote(src, dst, send, recv, target):
        return pltpu.make_async_remote_copy(
            src_ref=src, dst_ref=dst, send_sem=send, recv_sem=recv,
            device_id=target, device_id_type=MESH,
        )

    def ends(way, k):
        return k // 2 ^ way, k % 2

    def goes(d, way, k):
        return d < 4 or k < 2

    def w_goes(d, way, k):
        return d < 4 or k == way

    def tok_step(way, d, k):
        shard = (z - (d - 1)) % 8 if way == 0 else (z + (d - 1)) % 8
        target = device_z((z + 1) % 8 if way == 0 else (z + 7) % 8)
        part, side = ends(way, k)
        ref = tok.at[shard, part, side]
        return remote(
            ref, ref, tok_send.at[way, d - 1, k], tok_recv.at[way, d - 1, k], target
        )

    def swap_step(part):
        ref = tok.at[z, part, core]
        return remote(ref, ref, sib_send.at[0, part], sib_recv.at[0, part], sibling)

    def sib_step(way, d, k):
        slot = sib_slot(way, d)
        part, side = ends(way, k)
        ref = tok.at[(z - slot) % 8, part, side]
        c = part * 2 + side
        return remote(ref, ref, sib_send.at[slot, c], sib_recv.at[slot, c], sibling)

    def sib_slot(way, d):
        return d if way == 0 else 8 - d

    def half_of(k):
        return zl if k == 0 else 1 - zl

    def w_step(way, d, k):
        shard = (y - (d - 1)) % 8 if way == 0 else (y + (d - 1)) % 8
        target = device((y + 1) % 8 if way == 0 else (y + 7) % 8, zh, x, zl, core)
        ref = wbuf.at[shard, half_of(k)]
        return remote(
            ref, ref, wr_send.at[way, d - 1, k], wr_recv.at[way, d - 1, k], target
        )

    def ws_step(slot, k):
        ref = wbuf.at[(y - slot) % 8, half_of(k), 0]
        return remote(ref, ref, ws_send.at[slot, k], ws_recv.at[slot, k], sibling)

    def wa_step(k, owner):
        source = wown.at[:, half_of(k) * 2 + owner]
        landing = wbuf.at[y, zl, owner, core]
        slot = k * 2 + core
        return remote(
            source, landing, wa_send.at[k, owner], wa_recv.at[slot, owner],
            device(y, zh, x, half_of(k), 1),
        )

    def wa_arrival(k, side, owner):
        landing = wbuf.at[y, half_of(k), owner, side]
        return remote(
            landing, landing, wa_send.at[k, owner], wa_recv.at[k * 2 + side, owner], sibling
        )

    for copy in own_tok:
        copy.wait()
    for part in range(2):
        swap_step(part).start()

    @pl.when(core == 0)
    def _():
        for way in range(2):
            tok_step(way, 1, 0).start()

    own_w.wait()
    for owner in range(2):
        wa_step(1, owner).start()

    @pl.when(core == 0)
    def _():
        for owner in range(2):
            wa_step(0, owner).start()

    @pl.when(core == 1)
    def _():
        for owner in range(2):
            wbuf[y, zl, owner, 1] = wown[:, zl * 2 + owner]

    @pl.when(core == 0)
    def _():
        for part in range(2):
            swap_step(part).wait_recv()
        for k in range(1, 4):
            for way in range(2):
                tok_step(way, 1, k).start()

    @pl.when(core == 1)
    def _():
        for owner in range(2):
            wa_arrival(0, 0, owner).wait_recv()
        for way in range(2):
            w_step(way, 1, 0).start()
        ws_step(0, 0).start()

    for copy in own_filt:
        copy.wait()
    for k in range(4):
        tiles = [
            filt[j, pl.ds(k * 4 + ch, 8, stride=16), :]
            for ch in range(4)
            for j in range(2)
        ]
        fstage[k] = jnp.concatenate(tiles, 0).astype(BF16)
    for copy in own_params:
        copy.wait()
    pstage[...] = jnp.zeros_like(pstage)
    for i in range(3):
        for b in range(3):
            pstage[i * 3 + b : i * 3 + b + 1, :] = short[i, b : b + 1, :]
    pstage[9:10, :] = skip[...]

    def f_step(k):
        return remote(
            fstage.at[k], fmid.at[y], f_send.at[k], f_recv.at[0],
            device(4 * zl + k, zh, x, zl, core),
        )

    def g_step(i):
        return remote(
            fturn.at[i], fbuf.at[zh], g_send.at[i], g_recv.at[0], filter_holder(i)
        )

    def p_step(delta):
        mate = (quarter + delta) % 4
        return remote(
            pstage, pbuf, p_send.at[delta], p_recv.at[0], device(y, zh, x, mate // 2, mate % 2)
        )

    @pl.when(mirrored)
    def _():
        pltpu.make_async_copy(pstage, pbuf, p_recv.at[0]).start()
        for delta in range(1, 4):
            p_step(delta).start()

    def pass_tokens(d, k):
        for way in range(2):
            tok_step(way, d, k).wait_recv()
            if d < 4 and goes(d + 1, way, k):
                tok_step(way, d + 1, k).start()
            sib_step(way, d, k).start()

    def pass_weights(d, k):
        for way in range(2):
            if w_goes(d, way, k):
                w_step(way, d, k).wait_recv()
                if d < 4 and w_goes(d + 1, way, k):
                    w_step(way, d + 1, k).start()
                ws_step(sib_slot(way, d), k).start()

    def await_tokens(d):
        @pl.when(core == 1)
        def _():
            if d == 0:
                for part in range(2):
                    swap_step(part).wait_recv()
            else:
                for k in range(4):
                    for way in range(2):
                        if goes(d, way, k):
                            sib_step(way, d, k).wait_recv()

    def await_weights(d):
        @pl.when(core == 0)
        def _():
            for k in range(2):
                for way in range(2):
                    if w_goes(d, way, k) and (d > 0 or way == 0):
                        ws_step(sib_slot(way, d) % 8, k).wait_recv()

    @pl.when(core == 0)
    def _():
        for d in range(1, 3):
            for k in range(4):
                pass_tokens(d, k)

    @pl.when(core == 1)
    def _():
        for side in range(2):
            for owner in range(2):
                wa_arrival(1, side, owner).wait_recv()
        for way in range(2):
            w_step(way, 1, 1).start()
        ws_step(0, 1).start()
        for d in range(1, 4):
            for k in range(2):
                pass_weights(d, k)

    sign = 2 * zl - 1
    blocks = [zh, (zh + sign) % 4, (zh - sign) % 4, (zh + 2) % 4]
    near = [[0], [1, 7], [2, 6], [3, 5], [4]]

    def x_step(p, row):
        return remote(
            sbuf.at[p, row], rbuf.at[p, x, row % 2], x_send.at[p, row], x_recv.at[p],
            device(y, zh, row // 2, zl, core),
        )

    by_distance = [2 * ((x + hop) % 4) + part for hop in (2, 1, 3, 0) for part in range(2)]

    def project(p, steps):
        rows = [(y + delta) % 8 for step in steps for delta in near[step]]
        if len(rows) == 8:
            rows = by_distance
        total = jnp.zeros((48 * len(rows), 256), F32)
        for half in range(2):
            for side in range(2):
                left = jnp.concatenate(
                    [wbuf[row, half, core, side].reshape(48, 512) for row in rows], 0
                )
                right = tok[blocks[p] * 2 + half, :, side].reshape(256, 512)
                total = total + lax.dot_general(
                    left, right, (((1,), (1,)), ((), ())), preferred_element_type=F32
                )
        rounded = total.astype(BF16)
        for n, row in enumerate(rows):
            sbuf[p, row] = rounded[n * 48 : (n + 1) * 48, :]
        for row in rows:
            @pl.when(row // 2 != x)
            def _():
                x_step(p, row).start()

            @pl.when(row // 2 == x)
            def _():
                pltpu.make_async_copy(
                    sbuf.at[p, row], rbuf.at[p, x, row % 2], x_recv.at[p]
                ).start()

    def sum_over_x(p):
        pltpu.make_async_copy(rbuf.at[p], rbuf.at[p], x_recv.at[p]).wait()
        total = rbuf[p, 0].astype(F32)
        for n in range(1, 4):
            total = total + rbuf[p, n].astype(F32)
        total = total.reshape(96, 256)
        for j in range(2):
            sums[p, pl.ds(j, 96, stride=2), :] = total[:, j * 128 : (j + 1) * 128]

    def pieces(p, target):
        first_row = (target // 4) * 96 + (target % 4) * 8
        return [sums[p, first_row + b * 32 : first_row + b * 32 + 8, :] for b in range(3)]

    def e_step(delta):
        target = (y + delta) % 8
        return remote(
            aearly.at[target], xearly.at[y], e_send.at[delta], e_recv.at[0],
            device(target, zh, x, zl, core),
        )

    def a_step(delta):
        target = (y + delta) % 8
        return remote(
            alate.at[target], xlate.at[y], a_send.at[delta], a_recv.at[0],
            device(target, zh, x, zl, core),
        )

    def reduce_pair(first_block, packed, step, landed, arrived):
        for p in (first_block, first_block + 1):
            sum_over_x(p)
        for target in range(8):
            parts = pieces(first_block, target) + pieces(first_block + 1, target)
            packed[target] = jnp.concatenate(parts, 0).astype(BF16)
        for delta in FAR_FIRST:
            step(delta).start()
        pltpu.make_async_copy(packed.at[y], landed.at[y], arrived.at[0]).start()

    def reduce_early():
        reduce_pair(0, aearly, e_step, xearly, e_recv)

    def reduce_late():
        reduce_pair(2, alate, a_step, xlate, a_recv)

    def transform(value):
        stage = table_left(first[...], value)
        rows = []
        for ch in range(4):
            re = stage[:64, ch * 128 : (ch + 1) * 128]
            im = stage[64:, ch * 128 : (ch + 1) * 128]
            rows.append(
                jnp.concatenate(
                    [re * twist[0] + im * twist[1], im * twist[0] - re * twist[1]], 1
                )
            )
        return table_right(jnp.concatenate(rows, 0), second[...])

    @pl.when(core == 0)
    def _():
        for k in range(4):
            pass_tokens(3, k)

    await_tokens(0)
    await_tokens(1)
    for d in range(4):
        await_weights(d)
    project(0, [0, 1, 2, 3])
    await_tokens(2)
    project(1, [0, 1, 2, 3])

    @pl.when(core == 1)
    def _():
        for k in range(2):
            pass_weights(4, k)

    await_weights(4)
    for k in range(4):
        @pl.when(4 * zl + k != y)
        def _():
            f_step(k).start()

    @pl.when(between)
    def _():
        pltpu.make_async_copy(fstage.at[y % 4], fmid.at[y], f_recv.at[0]).start()

    project(0, [4])
    project(1, [4])
    await_tokens(3)
    project(2, [0, 1, 2, 3, 4])

    @pl.when(core == 0)
    def _():
        for k in range(2):
            pass_tokens(4, k)

    await_tokens(4)
    project(3, [0, 1, 2, 3, 4])
    @pl.when(between)
    def _():
        pltpu.make_async_copy(fmid, fmid, f_recv.at[0]).wait()
        fwide[...] = fmid[...].astype(F32).reshape(512, 128)
        for i in range(8):
            tiles = [fwide[pl.ds(n * 8 + i, 8, stride=64), :] for n in range(8)]
            fturn[i] = jnp.concatenate(tiles, 0).astype(BF16)
        for i in range(8):
            @pl.when(jnp.logical_not(at_home & (own_block == i)))
            def _():
                g_step(i).start()

        @pl.when(at_home)
        def _():
            pltpu.make_async_copy(fturn.at[own_block], fbuf.at[zh], g_recv.at[0]).start()

    reduce_early()

    reduce_late()

    @pl.when(core == 0)
    def _():
        for owner in range(2):
            wa_step(0, owner).wait_send()
        for d in range(1, 5):
            for k in range(4):
                for way in range(2):
                    if goes(d, way, k):
                        tok_step(way, d, k).wait_send()
                        sib_step(way, d, k).wait_send()

    @pl.when(core == 1)
    def _():
        for k in range(2):
            ws_step(0, k).wait_send()
        for d in range(1, 5):
            for k in range(2):
                for way in range(2):
                    if w_goes(d, way, k):
                        w_step(way, d, k).wait_send()
                        ws_step(sib_slot(way, d), k).wait_send()

    for owner in range(2):
        wa_step(1, owner).wait_send()
        swap_step(owner).wait_send()
    for p in range(4):
        for row in range(8):
            @pl.when(row // 2 != x)
            def _():
                x_step(p, row).wait_send()

    pltpu.make_async_copy(fbuf, fbuf, g_recv.at[0]).wait()
    pltpu.make_async_copy(pbuf, pbuf, p_recv.at[0]).wait()
    for copy in own_tables:
        copy.wait()
    wide = fbuf[...].astype(F32)
    lanes = []
    for ch in range(4):
        lanes.append(
            jnp.concatenate(
                [wide[n, (ch * 2 + j) * 8 : (ch * 2 + j + 1) * 8, :] for n in range(4) for j in range(2)],
                0,
            )
        )
    spectrum[...] = transform(jnp.concatenate(lanes, 1)) * (1.0 / 8192.0)

    for delta in FAR_FIRST:
        e_step(delta).wait_send()

    @pl.when(mirrored)
    def _():
        for delta in range(1, 4):
            p_step(delta).wait_send()

    for k in range(4):
        @pl.when(4 * zl + k != y)
        def _():
            f_step(k).wait_send()

    for i in range(8):
        @pl.when(between & jnp.logical_not(at_home & (own_block == i)))
        def _():
            g_step(i).wait_send()

    channel = 64 * (zh % 2) + 32 * zl + 16 * core + 4 * (y % 4)
    lane_at = lax.broadcasted_iota(jnp.int32, (16, 128), 1)
    gains = [
        jnp.sum(jnp.where(lane_at == channel + ch, pbuf[...], 0.0), axis=1, keepdims=True)
        for ch in range(4)
    ]
    pltpu.make_async_copy(xearly, xearly, e_recv.at[0]).wait()
    wide = xearly[...].astype(F32)
    for p in range(2):
        xwide[blocks[p]] = wide[:, p * 24 : (p + 1) * 24, :].reshape(192, 128)
    pltpu.make_async_copy(xlate, xlate, a_recv.at[0]).wait()
    wide = xlate[...].astype(F32)
    for p in range(2):
        xwide[blocks[2 + p]] = wide[:, p * 24 : (p + 1) * 24, :].reshape(192, 128)
    lane = lax.broadcasted_iota(jnp.int32, (64, 128), 1)
    below = lax.broadcasted_iota(jnp.int32, (8, 128), 0)

    def mixed(b, ch):
        here = jnp.concatenate(
            [
                xwide[inner // 2, pl.ds((b * 4 + ch) * 2 + inner % 2, 8, stride=24), :]
                for inner in range(8)
            ],
            0,
        )
        total = gains[ch][b : b + 1, :] * here
        for i in range(1, 3):
            turned = pltpu.roll(here, i, 1)
            wrapped = jnp.where(below == 0, 0.0, pltpu.roll(turned[56:, :], 1, 0))
            before = jnp.concatenate([wrapped, turned[:56, :]], 0)
            total = total + gains[ch][i * 3 + b : i * 3 + b + 1, :] * jnp.where(
                lane < i, before, turned
            )
        return total

    drives = [mixed(1, ch) * mixed(2, ch) for ch in range(4)]
    wave = transform(jnp.concatenate(drives, 1))
    wave_re, wave_im = wave[:, :128], wave[:, 128:]
    filt_re, filt_im = spectrum[:, :128], spectrum[:, 128:]
    product = jnp.concatenate(
        [wave_re * filt_re - wave_im * filt_im, wave_re * filt_im + wave_im * filt_re], 1
    )
    back = table_right(product, jnp.transpose(second[...], (1, 0)))
    columns = []
    for ch in range(4):
        re = back[ch * 64 : (ch + 1) * 64, :128]
        im = back[ch * 64 : (ch + 1) * 64, 128:]
        columns.append(
            jnp.concatenate(
                [re * twist[0] - im * twist[1], im * twist[0] + re * twist[1]], 0
            )
        )
    convolved = table_left(last[...], jnp.concatenate(columns, 1))
    for ch in range(4):
        gated = mixed(0, ch) * (
            convolved[:, ch * 128 : (ch + 1) * 128] + gains[ch][9:10, :] * drives[ch]
        )
        for inner in range(8):
            owide[pl.ds(ch * 8 + inner, 8, stride=32), :] = gated[
                inner * 8 : (inner + 1) * 8, :
            ]

    oturn[...] = owide[...].astype(BF16).reshape(8, 32, 128)

    def n_step(delta):
        target = (y + delta) % 8
        return remote(
            oturn.at[target], omid.at[y], n_send.at[delta], n_recv.at[0],
            device(target, zh, x, zl, core),
        )

    for delta in FAR_FIRST:
        n_step(delta).start()
    pltpu.make_async_copy(oturn.at[y], omid.at[y], n_recv.at[0]).start()

    out_rows = out.at[pl.ds(pl.multiple_of(own_block * 16, 16), 16)]

    def o_step(i):
        return remote(ostage.at[i], out_rows, o_send.at[i], o_recv.at[0], out_owner(i))

    pltpu.make_async_copy(omid, omid, n_recv.at[0]).wait()
    owide[...] = omid[...].astype(F32).reshape(256, 128)
    for i in range(8):
        first_row = (i // 4) * 128 + (i % 4) * 2
        ostage[i] = jnp.concatenate(
            [owide[pl.ds(first_row + j, 16, stride=8), :] for j in range(2)], 1
        ).astype(BF16)
    for i in range(8):
        @pl.when(jnp.logical_not(at_home & (own_out == i)))
        def _():
            o_step(i).start()

    @pl.when(at_home)
    def _():
        pltpu.make_async_copy(ostage.at[own_out], out_rows, o_recv.at[0]).start()

    for i in range(8):
        @pl.when(jnp.logical_not(at_home & (own_out == i)))
        def _():
            o_step(i).wait_send()

    for delta in FAR_FIRST:
        a_step(delta).wait_send()
        n_step(delta).wait_send()
    pltpu.make_async_copy(out, out, o_recv.at[0]).wait()


def per_device(tokens, in_weight, short_filter, long_filter, skip_gain):
    consts = [jnp.asarray(table) for table in tables()]
    dma = pltpu.SemaphoreType.DMA
    hbm = pl.BlockSpec(memory_space=pltpu.HBM)
    columns = jnp.transpose(in_weight, (0, 2, 1)).reshape(3, 4, 16, 512)
    return pl.pallas_call(
        kernel,
        out_shape=jax.ShapeDtypeStruct((128, 256), BF16),
        in_specs=[hbm] * 9,
        out_specs=hbm,
        scratch_shapes=[
            pltpu.VMEM((128, 64), F32),
            pltpu.VMEM((2, 64, 128), F32),
            pltpu.VMEM((256, 256), F32),
            pltpu.VMEM((64, 128), F32),
            pltpu.VMEM((3, 3, 128), F32),
            pltpu.VMEM((1, 128), F32),
            pltpu.VMEM((2, 128, 128), F32),
            pltpu.VMEM((8, 2, 2, 128, 512), BF16),
            pltpu.VMEM((3, 4, 16, 512), BF16),
            pltpu.VMEM((8, 2, 2, 2, 3, 16, 512), BF16),
            pltpu.VMEM((4, 8, 48, 256), BF16),
            pltpu.VMEM((4, 4, 2, 48, 256), BF16),
            pltpu.VMEM((4, 192, 128), F32),
            pltpu.VMEM((8, 48, 128), BF16),
            pltpu.VMEM((8, 48, 128), BF16),
            pltpu.VMEM((8, 48, 128), BF16),
            pltpu.VMEM((8, 48, 128), BF16),
            pltpu.VMEM((4, 192, 128), F32),
            pltpu.VMEM((4, 64, 128), BF16),
            pltpu.VMEM((8, 64, 128), BF16),
            pltpu.VMEM((512, 128), F32),
            pltpu.VMEM((8, 64, 128), BF16),
            pltpu.VMEM((4, 64, 128), BF16),
            pltpu.VMEM((16, 128), F32),
            pltpu.VMEM((16, 128), F32),
            pltpu.VMEM((256, 256), F32),
            pltpu.VMEM((256, 128), F32),
            pltpu.VMEM((8, 32, 128), BF16),
            pltpu.VMEM((8, 32, 128), BF16),
            pltpu.VMEM((8, 16, 256), BF16),
            dma((2,)), dma((2,)), dma((1,)), dma((2,)), dma((4,)),
            dma((2, 4, 4)), dma((2, 4, 4)),
            dma((8, 4)), dma((8, 4)),
            dma((2, 2)), dma((4, 2)),
            dma((2, 4, 2)), dma((2, 4, 2)),
            dma((8, 2)), dma((8, 2)),
            dma((4, 8)), dma((4,)),
            dma((8,)), dma((1,)),
            dma((8,)), dma((1,)),
            dma((4,)), dma((1,)),
            dma((8,)), dma((1,)),
            dma((4,)), dma((1,)),
            dma((8,)), dma((1,)),
            dma((8,)), dma((1,)),
        ],
        compiler_params=pltpu.CompilerParams(
            collective_id=0, has_side_effects=True, vmem_limit_bytes=63 * 1024 * 1024
        ),
    )(tokens.reshape(2, 128, 512), columns, short_filter, long_filter, skip_gain[None, :], *consts)


def solution(mesh):
    placed = (
        P("seq", "chan"),
        P(None, "chan", "seq"),
        P(None, None, "chan"),
        P("chan", "seq"),
        P("chan"),
    )
    return jax.shard_map(
        per_device, mesh=mesh, in_specs=placed, out_specs=P("chan", "seq"), check_vma=False
    )
```
